256 devices in a mesh: ctx: 8 (over z), ch: 32 (over x, y, core).
Axes of the slice: x: 4, y: 4, z: 8, core: 2. Of those that a mesh axis runs over, the one named last changes fastest.
Arguments:
- u_rows: bfloat16 [16384, 8192], P(('ctx', 'ch')), may hold values from -6 to 6
- gain: float32 [8192], replicated, may hold values from 0.1 to 1.9
- skip: float32 [8192], P('ch'), may hold values from -4 to 4
- residues: float32 [8192, 16], P('ch'), may hold values from -1.5 to 1.5
- rates: float32 [8192, 16], P('ch'), may hold values from 1.8310547e-05 to 0.04
- grad_out: bfloat16 [16384, 8192], P('ctx', 'ch'), may hold values from -6 to 6
- doc_lengths: int32 [4], replicated, may hold values from 1 to 8192, 16384 in all
- doc_streams: int32 [4], replicated, may hold values from 0 to 1
Outputs:
- input_grad: bfloat16 [16384, 8192], P(('ctx', 'ch'))
- residue_grad: float32 [2, 8192, 16], P(None, 'ch')
The draws below stay inside these ranges and needn't reach their ends.
Inputs may be any that keep to these rules, and one draw needn't show every extreme that they name: `doc_lengths`: the lengths sum to 16384 and the largest is exactly 8192.
All inputs are finite; a program needn't handle non-finite values.
Results may differ from the reference program's by a relative error of at most 0.015.
Values may be sent and summed in bfloat16 or wider, within the bound.
No kernel may reach another device: no remote copies, remote signals or barrier semaphores. Data moves between devices by JAX's collectives and lax.ppermute only.
A program may use at most 64 MiB of HBM per device.

```python
import math
import jax
import jax.numpy as jnp
import numpy as np
from jax import lax

C = 8192
MODES = 16
NDOCS = 4
TOKENS = 16384


def draw_u_rows(key, part):
    key = jax.random.fold_in(key, 11)
    noise_key = jax.random.fold_in(key, 0)
    values = jax.random.truncated_normal(noise_key, -6.0, 6.0, (TOKENS, C), jnp.float32)
    return values.astype(jnp.bfloat16)


def draw_grad_out(key, part):
    key = jax.random.fold_in(key, 17)
    noise_key = jax.random.fold_in(key, 0)
    values = jax.random.truncated_normal(noise_key, -6.0, 6.0, (TOKENS, C), jnp.float32)
    return values.astype(jnp.bfloat16)


def draw_rates(key, part):
    key = jax.random.fold_in(key, 23)
    lowest = math.log(0.3 / TOKENS)
    highest = math.log(0.04)
    spread = jax.random.uniform(key, (C, MODES), jnp.float32, lowest, highest)
    return jnp.exp(spread).astype(jnp.float32)


def with_ends(values, own_key, smallest, high):
    place = [jax.random.randint(jax.random.fold_in(own_key, axis), (), 0, length) for axis, length in enumerate(values.shape)]
    main_axis = values.shape.index(max(values.shape))
    next_to = place[:main_axis] + [(place[main_axis] + 1) % values.shape[main_axis]] + place[main_axis + 1:]
    return values.at[tuple(place)].set(smallest).at[tuple(next_to)].set(high)


def levels(key, shape, shards, smallest, top_value):
    level = 1.0
    for dim, blocks in shards:
        draws = jax.random.uniform(jax.random.fold_in(jax.random.fold_in(key, 6), dim), (blocks,), jnp.float32, smallest / len(shards), top_value / len(shards))
        level = level * jnp.repeat(jnp.exp(draws), shape[dim] // blocks).reshape((-1,) + (1,) * (len(shape) - 1 - dim))
    return level


def split_up(amount, total, reach, lean):
    loads = [(1 << 20) // math.isqrt(grade ** lean) + 1 for grade in range(2, amount + 1)]
    spare, given = total - reach - (amount - 1), [1] * (amount - 1)
    while spare > 0:
        candidates = [i for i in range(amount - 1) if given[i] < reach]
        whole, budget = sum([loads[i] for i in candidates]), spare
        for i in candidates:
            addition = min(reach - given[i], max(1, budget * loads[i] // whole), spare)
            given[i] = given[i] + addition
            spare = spare - addition
    return np.array([reach] + given)


def uneven(own_key, count, total, bound, skew):
    if count == 2:
        one = jax.random.randint(own_key, (), max(1, total - bound), min(bound, total - 1) + 1)
        return jnp.stack([one, total - one])
    lengths = jnp.asarray(split_up(count, total, bound, skew), jnp.int32)
    pairs = (count - 1) // 2
    source_of, taker = lengths[1:1 + 2 * pairs:2], lengths[2:2 + 2 * pairs:2]
    margin = jnp.minimum(source_of - 1, bound - taker)
    moved = jax.random.randint(jax.random.fold_in(own_key, 1), (pairs,), 0, 1 << 20) % (margin + 1)
    lengths = lengths.at[1:1 + 2 * pairs:2].set(source_of - moved).at[2:2 + 2 * pairs:2].set(taker + moved)
    return lengths[jax.random.permutation(jax.random.fold_in(own_key, 2), count)]


def normal_values(key, shape, deviation, reach, pieces=(), kind=jnp.bfloat16):
    level = levels(key, shape, pieces, -0.22, 0.18) if pieces else 1.0
    values = jax.random.normal(key, shape, jnp.float32) * deviation * level
    return jnp.minimum(jnp.maximum(values, -reach), reach).astype(kind)


def setup_inputs(seed: int = 0) -> dict:
    key_list = jax.random.split(jax.random.key(seed), 9)
    u_rows = draw_u_rows(jax.random.fold_in(key_list[8], 71), 0)
    gain = jnp.clip(1.0 + 0.18 * jax.random.normal(key_list[1], (C,), jnp.float32), 0.1, 1.9)
    skip = normal_values(key_list[2], (C,), 1.0, 4.0, ((0, 32),), jnp.float32)
    residues = normal_values(key_list[3], (C, MODES), MODES ** -0.5, 1.5, ((0, 32),), jnp.float32)
    rates = draw_rates(jax.random.fold_in(key_list[8], 71), 0)
    grad_out = draw_grad_out(jax.random.fold_in(key_list[8], 71), 0)
    doc_lengths = uneven(key_list[6], NDOCS, TOKENS, TOKENS // 2, 2).astype(jnp.int32)
    doc_streams = with_ends(jax.random.randint(key_list[7], (NDOCS,), 0, 2), jax.random.fold_in(key_list[7], 1), 0, 1).astype(jnp.int32)
    return {"u_rows": u_rows, "gain": gain, "skip": skip, "residues": residues, "rates": rates, "grad_out": grad_out, "doc_lengths": doc_lengths, "doc_streams": doc_streams}


def token_tables(doc_lengths, doc_streams, positions):
    starts = jnp.cumsum(doc_lengths) - doc_lengths
    start_flag = jnp.any(positions[:, None] == starts[None, :], axis=1).astype(jnp.float32)
    document = lax.optimization_barrier(jnp.sum((positions[:, None] >= starts[None, :]).astype(jnp.int32), axis=1)) - 1
    doc_total = doc_lengths.shape[0]
    member = (document[:, None] == jnp.arange(doc_total, dtype=jnp.int32)[None, :]).astype(jnp.int32)
    stream = lax.optimization_barrier(jnp.sum(member * doc_streams[None, :], axis=1))
    onehot = (stream[:, None] == jnp.arange(2, dtype=jnp.int32)[None, :]).astype(jnp.float32)
    return (start_flag, onehot)

def reference(u_rows, gain, skip, residues, rates, grad_out, doc_lengths, doc_streams):
    u_float = u_rows.astype(jnp.float32)
    inv_rms = lax.rsqrt(lax.optimization_barrier(jnp.mean(u_float * u_float, axis=1)) + 1e-05)
    normal_u = u_float * inv_rms[:, None]
    normed = (normal_u * gain[None, :]).astype(jnp.bfloat16)
    decay = jnp.exp(-rates)
    mode_scale = jnp.sqrt(1.0 - decay * decay)
    mode_weight = residues * mode_scale
    positions = jnp.arange(TOKENS, dtype=jnp.int32)
    start_flag, onehot = token_tables(doc_lengths, doc_streams, positions)
    keep = 1.0 - start_flag
    group_width = math.gcd(C, 256)
    groups = C // group_width

    def split(array):
        return array.reshape(TOKENS, groups, group_width).transpose(1, 0, 2)

    def one_group(operands):
        x_group, dy_group, decay_group, weight_group = operands
        zero_state = jnp.zeros(decay_group.shape, jnp.float32)

        def forward(carry, row):
            state, total = carry
            x_row, dy_row, keep_row, pick = row
            state = x_row.astype(jnp.float32)[:, None] + decay_group * keep_row * state
            total = total + pick[:, None, None] * (dy_row.astype(jnp.float32)[:, None] * state)[None]
            return ((state, total), None)
        start_total = jnp.zeros((2,) + decay_group.shape, jnp.float32)
        (_, total), _ = lax.scan(forward, (zero_state, start_total), (x_group, dy_group, keep, onehot))

        def backward(carry, row):
            dy_row, keep_row = row
            state = dy_row.astype(jnp.float32)[:, None] + carry
            return (decay_group * keep_row * state, lax.optimization_barrier(jnp.sum(weight_group * state, axis=1)))
        _, conv_grad = lax.scan(backward, zero_state, (dy_group, keep), reverse=True)
        return (total, conv_grad)
    totals, conv_grads = lax.map(one_group, (split(normed), split(grad_out), decay.reshape(groups, group_width, MODES), mode_weight.reshape(groups, group_width, MODES)))
    residue_grad = totals.transpose(1, 0, 2, 3).reshape(2, C, MODES) * mode_scale[None] / math.sqrt(TOKENS)
    conv_grad = conv_grads.transpose(1, 0, 2).reshape(TOKENS, C)
    normed_grad = (skip[None, :] * grad_out.astype(jnp.float32) + conv_grad).astype(jnp.bfloat16)
    scaled = gain[None, :] * normed_grad.astype(jnp.float32)
    project = lax.optimization_barrier(jnp.mean(normal_u * scaled, axis=1))
    input_grad = (inv_rms[:, None] * (scaled - normal_u * project[:, None])).astype(jnp.bfloat16)
    return (input_grad, residue_grad)
```

```python
import math

import jax
import jax.numpy as jnp
from jax import lax
from jax.experimental import pallas as pl
from jax.experimental.pallas import tpu as pltpu
from jax.sharding import PartitionSpec as P

F32 = jnp.float32
BF16 = jnp.bfloat16
SEGS = 8
LANES = 128
UNROLL = 8
ROW_BLOCK = 16


def params(limit=32 * 1024 * 1024):
    return pltpu.CompilerParams(vmem_limit_bytes=limit)


def vmem():
    return pl.BlockSpec(memory_space=pltpu.VMEM)


def smem():
    return pl.BlockSpec(memory_space=pltpu.SMEM)


def cost(flops, size):
    return pl.CostEstimate(flops=flops, bytes_accessed=size, transcendentals=0)


def inverse_rms(u_ref, eps=1e-05):
    rows, width = u_ref.shape
    total = jnp.zeros((rows, LANES), F32)
    for c in range(width // LANES):
        part = u_ref[:, c * LANES : (c + 1) * LANES].astype(F32)
        total = total + part * part
    return lax.rsqrt(jnp.sum(total, axis=1, keepdims=True) / width + eps)


def norm_kernel(u_ref, gain_ref, out_ref):
    groups, _, chans = out_ref.shape
    inv = inverse_rms(u_ref)
    for c in range(groups):
        cols = slice(c * chans, (c + 1) * chans)
        normal = u_ref[:, cols].astype(F32) * inv
        out_ref[c] = (normal * gain_ref[:, cols]).astype(BF16)


def norm_rows(u_rows, gain, groups):
    rows, width = u_rows.shape
    chans = width // groups
    return pl.pallas_call(
        norm_kernel,
        grid=(rows // ROW_BLOCK,),
        in_specs=[
            pl.BlockSpec((ROW_BLOCK, width), lambda i: (i, 0)),
            pl.BlockSpec((1, width), lambda i: (0, 0)),
        ],
        out_specs=pl.BlockSpec((groups, ROW_BLOCK, chans), lambda i: (0, i, 0)),
        out_shape=jax.ShapeDtypeStruct((groups, rows, chans), BF16),
        compiler_params=params(),
        cost_estimate=cost(8 * rows * width, 4 * rows * width),
        name="norm_rows",
    )(u_rows, gain)


def final_kernel(u_ref, gain_ref, grad_ref, out_ref):
    groups, rows, chans = grad_ref.shape
    width = groups * chans
    inv = inverse_rms(u_ref)
    total = jnp.zeros((rows, chans), F32)
    for c in range(groups):
        cols = slice(c * chans, (c + 1) * chans)
        normal = u_ref[:, cols].astype(F32) * inv
        total = total + normal * (gain_ref[:, cols] * grad_ref[c].astype(F32))
    project = jnp.sum(total, axis=1, keepdims=True) / width
    for c in range(groups):
        cols = slice(c * chans, (c + 1) * chans)
        normal = u_ref[:, cols].astype(F32) * inv
        scaled = gain_ref[:, cols] * grad_ref[c].astype(F32)
        out_ref[:, cols] = (inv * (scaled - normal * project)).astype(BF16)


def final_rows(u_rows, gain, grad_rows):
    rows, width = u_rows.shape
    groups, _, chans = grad_rows.shape
    return pl.pallas_call(
        final_kernel,
        grid=(rows // ROW_BLOCK,),
        in_specs=[
            pl.BlockSpec((ROW_BLOCK, width), lambda i: (i, 0)),
            pl.BlockSpec((1, width), lambda i: (0, 0)),
            pl.BlockSpec((groups, ROW_BLOCK, chans), lambda i: (0, i, 0)),
        ],
        out_specs=pl.BlockSpec((ROW_BLOCK, width), lambda i: (i, 0)),
        out_shape=jax.ShapeDtypeStruct((rows, width), BF16),
        compiler_params=params(),
        cost_estimate=cost(16 * rows * width, 6 * rows * width),
        name="final_rows",
    )(u_rows, gain, grad_rows)


def doc_starts(lens_ref):
    starts, at = [], jnp.int32(0)
    for k in range(lens_ref.shape[0] - 1):
        at = at + lens_ref[k]
        starts.append(at)
    return starts


def sort_down(codes):
    codes = list(codes)
    for end in range(len(codes) - 1, 0, -1):
        for k in range(end):
            high = jnp.maximum(codes[k], codes[k + 1])
            low = jnp.minimum(codes[k], codes[k + 1])
            codes[k], codes[k + 1] = high, low
    return codes


def cut_codes(starts, streams, base, seg_len):
    codes = []
    for start, stream in zip(starts, streams):
        place = start - base
        inside = (place >= 0) & (place < SEGS * seg_len)
        code = (place % seg_len) * 16 + place // seg_len
        codes.append(jnp.where(inside, code, 15) * 2 + stream)
    return sort_down(codes)


def any_start(starts, first, count):
    found = jnp.bool_(False)
    for start in starts:
        found = found | ((start >= first) & (start < first + count))
    return found


def time_loop(cuts_ref, seg_len, step, cut, carry):
    def piece(p, state):
        top, inner = state
        code = cuts_ref[p]
        low = code // 32
        count = top - low
        full = count // UNROLL

        def many(k, value):
            first = top - (k + 1) * UNROLL
            for j in range(UNROLL - 1, -1, -1):
                value = step(first + j, value)
            return value

        def one(k, value):
            return step(top - full * UNROLL - 1 - k, value)

        inner = lax.fori_loop(0, full, many, inner)
        inner = lax.fori_loop(0, count - full * UNROLL, one, inner)
        inner = cut((code // 2) % 16, code % 2, inner)
        return (low, inner)

    return lax.fori_loop(0, cuts_ref.shape[0], piece, (jnp.int32(seg_len), carry))[1]


def widen(source_ref, target_ref, chunk=64):
    def body(k, _):
        rows = pl.ds(k * chunk, chunk)
        for h in range(target_ref.shape[0]):
            target_ref[h, rows, :] = source_ref[rows, h * LANES : (h + 1) * LANES].astype(F32)
        return 0

    lax.fori_loop(0, source_ref.shape[0] // chunk, body, 0)


def spread(ref, r, cols):
    return jnp.broadcast_to(ref[r : r + 1, cols], (SEGS, LANES))


def segment(ref, s, modes):
    rows = slice(s * modes, (s + 1) * modes)
    return jnp.concatenate([ref[h, rows, :] for h in range(ref.shape[0])], axis=1)


def put_segment(ref, s, modes, value):
    for h in range(ref.shape[0]):
        ref[h, s * modes : (s + 1) * modes, :] = value[:, h * LANES : (h + 1) * LANES]


def store_cuts(cuts_ref, codes):
    for k, code in enumerate(codes):
        cuts_ref[k] = code
    cuts_ref[len(codes)] = jnp.int32(30)


def leave_kernel(lens_ref, rates_ref, grad_ref, seg_ref, dev_ref, wide_ref, decay_ref, cuts_ref):
    tokens, chans = grad_ref.shape
    modes = rates_ref.shape[0]
    seg_len = tokens // SEGS
    base = lax.axis_index("ctx") * tokens
    starts = doc_starts(lens_ref)
    store_cuts(cuts_ref, cut_codes(starts, [0] * len(starts), base, seg_len))
    decay_ref[...] = jnp.exp(-rates_ref[...])
    widen(grad_ref, wide_ref)
    row = lax.broadcasted_iota(jnp.int32, (SEGS, LANES), 0)
    for h in range(chans // LANES):
        cols = slice(h * LANES, (h + 1) * LANES)
        decay = [spread(decay_ref, r, cols) for r in range(modes)]

        def step(i, state):
            grad = wide_ref[h, pl.ds(i, SEGS, stride=seg_len), :]
            return tuple(grad + decay[r] * state[r] for r in range(modes))

        def cut(segment, stream, state):
            hold = row != segment
            return tuple(jnp.where(hold, part, 0.0) for part in state)

        zero = jnp.zeros((SEGS, LANES), F32)
        state = time_loop(cuts_ref, seg_len, step, cut, (zero,) * modes)
        for r in range(modes):
            seg_ref[h, pl.ds(r, SEGS, stride=modes), :] = decay[r] * state[r]
    through = jnp.exp(-rates_ref[...] * float(seg_len))
    leaving = segment(seg_ref, SEGS - 1, modes)
    for s in range(SEGS - 2, -1, -1):
        kept = jnp.where(any_start(starts, base + s * seg_len, seg_len), 0.0, 1.0)
        leaving = segment(seg_ref, s, modes) + (through * kept) * leaving
    for k in range(dev_ref.shape[0]):
        dev_ref[k] = leaving


def leave(doc_lengths, rates, grad_out, copies):
    modes, chans = rates.shape
    tokens = grad_out.shape[0]
    return pl.pallas_call(
        leave_kernel,
        in_specs=[smem(), vmem(), vmem()],
        out_specs=[vmem(), vmem()],
        out_shape=[
            jax.ShapeDtypeStruct((chans // LANES, SEGS * modes, LANES), F32),
            jax.ShapeDtypeStruct((copies, modes, chans), F32),
        ],
        scratch_shapes=[
            pltpu.VMEM((chans // LANES, tokens, LANES), F32),
            pltpu.VMEM((modes, chans), F32),
            pltpu.SMEM((doc_lengths.shape[0],), jnp.int32),
        ],
        compiler_params=params(),
        cost_estimate=cost(2 * tokens * chans * modes, 2 * tokens * chans),
        name="leave",
    )(doc_lengths, rates, grad_out)


def back_kernel(
    lens_ref, rates_ref, residues_ref, skip_ref, grad_ref, seg_ref, dev_ref,
    out_ref, arrive_ref, wide_ref, conv_ref, decay_ref, weight_ref, cuts_ref,
):
    tokens, chans = grad_ref.shape
    modes = rates_ref.shape[0]
    seg_len = tokens // SEGS
    here = lax.axis_index("ctx")
    base = here * tokens
    starts = doc_starts(lens_ref)
    store_cuts(cuts_ref, cut_codes(starts, [0] * len(starts), base, seg_len))
    rates = rates_ref[...]
    decay_all = jnp.exp(-rates)
    decay_ref[...] = decay_all
    weight_ref[...] = residues_ref[...] * jnp.sqrt(1.0 - decay_all * decay_all)
    through = jnp.exp(-rates * float(tokens))
    arriving = jnp.zeros((modes, chans), F32)
    for k in range(dev_ref.shape[0] - 1, 0, -1):
        kept = jnp.where(any_start(starts, k * tokens, tokens), 0.0, 1.0)
        arriving = jnp.where(k > here, dev_ref[k] + (through * kept) * arriving, arriving)
    through = jnp.exp(-rates * float(seg_len))
    put_segment(arrive_ref, SEGS - 1, modes, arriving)
    for s in range(SEGS - 1, 0, -1):
        kept = jnp.where(any_start(starts, base + s * seg_len, seg_len), 0.0, 1.0)
        arriving = segment(seg_ref, s, modes) + (through * kept) * arriving
        put_segment(arrive_ref, s - 1, modes, arriving)
    widen(grad_ref, wide_ref)
    row = lax.broadcasted_iota(jnp.int32, (SEGS, LANES), 0)
    for h in range(chans // LANES):
        cols = slice(h * LANES, (h + 1) * LANES)
        decay = [spread(decay_ref, r, cols) for r in range(modes)]
        weight = [spread(weight_ref, r, cols) for r in range(modes)]
        skip = jnp.broadcast_to(skip_ref[:, cols], (SEGS, LANES))

        def step(i, state):
            rows = pl.ds(i, SEGS, stride=seg_len)
            grad = wide_ref[h, rows, :]
            back = tuple(grad + part for part in state)
            terms = [weight[r] * back[r] for r in range(modes)] + [skip * grad]
            while len(terms) > 1:
                terms = [a + b for a, b in zip(terms[::2], terms[1::2])] + terms[len(terms) // 2 * 2 :]
            conv_ref[h, rows, :] = terms[0]
            return tuple(decay[r] * back[r] for r in range(modes))

        def cut(segment, stream, state):
            hold = row != segment
            return tuple(jnp.where(hold, part, 0.0) for part in state)

        entry = tuple(arrive_ref[h, pl.ds(r, SEGS, stride=modes), :] for r in range(modes))
        time_loop(cuts_ref, seg_len, step, cut, entry)

    def narrow(k, _):
        rows = pl.ds(k * 64, 64)
        for h in range(conv_ref.shape[0]):
            out_ref[rows, h * LANES : (h + 1) * LANES] = conv_ref[h, rows, :].astype(BF16)
        return 0

    lax.fori_loop(0, tokens // 64, narrow, 0)


def back_pass(doc_lengths, rates, residues, skip, grad_out, seg_leaving, dev_leaving):
    modes, chans = rates.shape
    tokens = grad_out.shape[0]
    return pl.pallas_call(
        back_kernel,
        in_specs=[smem()] + [vmem()] * 6,
        out_specs=[vmem(), vmem()],
        out_shape=[
            jax.ShapeDtypeStruct((tokens, chans), BF16),
            jax.ShapeDtypeStruct((chans // LANES, SEGS * modes, LANES), F32),
        ],
        scratch_shapes=[
            pltpu.VMEM((chans // LANES, tokens, LANES), F32),
            pltpu.VMEM((chans // LANES, tokens, LANES), F32),
            pltpu.VMEM((modes, chans), F32),
            pltpu.VMEM((modes, chans), F32),
            pltpu.SMEM((doc_lengths.shape[0],), jnp.int32),
        ],
        compiler_params=params(),
        cost_estimate=cost(4 * tokens * chans * modes, 4 * tokens * chans),
        name="back_pass",
    )(doc_lengths, rates, residues, skip, grad_out, seg_leaving, dev_leaving)


def residue_kernel(
    window, lens_ref, streams_ref, rates_ref, grad_ref, x_ref, arrive_ref,
    out_ref, wide_ref, x_wide_ref, decay_ref, total_ref, cuts_ref,
):
    tokens, chans = grad_ref.shape
    modes = rates_ref.shape[0]
    seg_len = tokens // SEGS
    base = lax.axis_index("ctx") * tokens
    starts = doc_starts(lens_ref)
    streams = [streams_ref[k] for k in range(len(starts) + 1)]
    store_cuts(cuts_ref, cut_codes(starts, streams[1:], base, seg_len))
    decay_all = jnp.exp(-rates_ref[...])
    decay_ref[...] = decay_all
    widen(grad_ref, wide_ref)
    widen(x_ref, x_wide_ref)
    total_ref[...] = jnp.zeros_like(total_ref)
    row = lax.broadcasted_iota(jnp.int32, (SEGS, LANES), 0)
    first = base + row * seg_len
    stream_at = jnp.full((SEGS, LANES), streams[0], jnp.int32)
    for start, stream in zip(starts, streams[1:]):
        stream_at = jnp.where(first >= start, stream, stream_at)
    for h in range(chans // LANES):
        cols = slice(h * LANES, (h + 1) * LANES)
        decay = [spread(decay_ref, r, cols) for r in range(modes)]

        def step(i, carry):
            state, total = carry
            rows = pl.ds(i, SEGS, stride=seg_len)
            grad = wide_ref[h, rows, :]
            x = x_wide_ref[h, rows, :]
            back = tuple(grad + part for part in state)
            total = tuple(total[r] + x * back[r] for r in range(modes))
            return (tuple(decay[r] * back[r] for r in range(modes)), total)

        def cut(segment, stream, carry):
            state, total = carry
            hold = row != segment
            for r in range(modes):
                total_ref[stream, r, :, cols] += jnp.where(hold, 0.0, total[r])
            return (
                tuple(jnp.where(hold, part, 0.0) for part in state),
                tuple(jnp.where(hold, part, 0.0) for part in total),
            )

        zero = jnp.zeros((SEGS, LANES), F32)
        entry = tuple(arrive_ref[h, pl.ds(r, SEGS, stride=modes), :] for r in range(modes))
        _, total = time_loop(cuts_ref, seg_len, step, cut, (entry, (zero,) * modes))
        for s in range(2):
            for r in range(modes):
                total_ref[s, r, :, cols] += jnp.where(stream_at == s, total[r], 0.0)
    scale = jnp.sqrt(1.0 - decay_all * decay_all) / math.sqrt(window)
    for s in range(2):
        part = (jnp.sum(total_ref[s], axis=1) * scale).astype(BF16)
        for k in range(out_ref.shape[0]):
            out_ref[k, s] = part


def residue_pass(doc_lengths, doc_streams, rates, grad_out, x_cols, arriving, copies, window):
    modes, chans = rates.shape
    tokens = grad_out.shape[0]

    def kernel(*refs):
        residue_kernel(window, *refs)

    return pl.pallas_call(
        kernel,
        in_specs=[smem(), smem()] + [vmem()] * 4,
        out_specs=vmem(),
        out_shape=jax.ShapeDtypeStruct((copies, 2, modes, chans), BF16),
        scratch_shapes=[
            pltpu.VMEM((chans // LANES, tokens, LANES), F32),
            pltpu.VMEM((chans // LANES, tokens, LANES), F32),
            pltpu.VMEM((modes, chans), F32),
            pltpu.VMEM((2, modes, SEGS, chans), F32),
            pltpu.SMEM((doc_lengths.shape[0],), jnp.int32),
        ],
        compiler_params=params(),
        cost_estimate=cost(4 * tokens * chans * modes, 4 * tokens * chans),
        name="residue_pass",
    )(doc_lengths, doc_streams, rates, grad_out, x_cols, arriving)


def local(u_rows, gain, skip, residues, rates, grad_out, doc_lengths, doc_streams):
    ctx, groups = lax.axis_size("ctx"), lax.axis_size("ch")
    tokens, chans = grad_out.shape
    gain = gain[None, :]
    rates, residues = rates.T, residues.T
    x_send = norm_rows(u_rows, gain, groups)
    x_cols = lax.all_to_all(x_send, "ch", split_axis=0, concat_axis=0, tiled=True)
    x_cols = x_cols.reshape(tokens, chans)
    seg_leaving, dev_leaving = leave(doc_lengths, rates, grad_out, ctx)
    dev_leaving = lax.all_to_all(dev_leaving, "ctx", split_axis=0, concat_axis=0, tiled=True)
    normed_grad, arriving = back_pass(
        doc_lengths, rates, residues, skip[None, :], grad_out, seg_leaving, dev_leaving
    )
    grad_rows = lax.all_to_all(
        normed_grad.reshape(groups, tokens // groups, chans), "ch", split_axis=0, concat_axis=0, tiled=True
    )
    parts = residue_pass(
        doc_lengths, doc_streams, rates, grad_out, x_cols, arriving, ctx, tokens * ctx
    )
    parts = lax.all_to_all(parts, "ctx", split_axis=0, concat_axis=0, tiled=True)
    residue_grad = jnp.sum(parts.astype(F32), axis=0).transpose(0, 2, 1)
    input_grad = final_rows(u_rows, gain, grad_rows)
    return (input_grad, residue_grad)


def solution(mesh):
    return jax.shard_map(
        local,
        mesh=mesh,
        in_specs=(
            P(("ctx", "ch"), None),
            P(),
            P("ch"),
            P("ch", None),
            P("ch", None),
            P("ctx", "ch"),
            P(),
            P(),
        ),
        out_specs=(P(("ctx", "ch"), None), P(None, "ch", None)),
        check_vma=False,
    )
```

```python
import math

import jax
import jax.numpy as jnp
from jax import lax
from jax.experimental import pallas as pl
from jax.experimental.pallas import tpu as pltpu
from jax.sharding import PartitionSpec as P

F32 = jnp.float32
BF16 = jnp.bfloat16
SEGS = 8
LANES = 128
UNROLL = 8
PIECES = 4
ROW_BLOCK = 16


def cost(flops, size):
    return pl.CostEstimate(flops=flops, bytes_accessed=size, transcendentals=0)


def load(pairs, sems):
    copies = [pltpu.make_async_copy(a, b, sems.at[k]) for k, (a, b) in enumerate(pairs)]
    for copy in copies:
        copy.start()
    return copies


def call(kernel, outs, scratch, sems, name, estimate, *operands):
    return pl.pallas_call(
        kernel,
        in_specs=[pl.BlockSpec(memory_space=pl.ANY)] * len(operands),
        out_specs=[pl.BlockSpec(memory_space=pl.ANY)] * len(outs),
        out_shape=outs,
        scratch_shapes=scratch + [pltpu.SemaphoreType.DMA((sems,))],
        compiler_params=pltpu.CompilerParams(vmem_limit_bytes=60 * 1024 * 1024),
        cost_estimate=estimate,
        name=name,
    )(*operands)


def inverse_rms(u_ref, eps=1e-05):
    rows, width = u_ref.shape
    total = jnp.zeros((rows, LANES), F32)
    for c in range(width // LANES):
        part = u_ref[:, c * LANES : (c + 1) * LANES].astype(F32)
        total = total + part * part
    return lax.rsqrt(jnp.sum(total, axis=1, keepdims=True) / width + eps)


def norm_kernel(u_hbm, gain_hbm, out_hbm, u_ref, gain_ref, out_ref, sems):
    blocks, groups, rows, chans = out_ref.shape
    span = [pl.ds(b * rows, rows) for b in range(blocks)]
    gain_copy, *u_copies = load(
        [(gain_hbm, gain_ref)] + [(u_hbm.at[span[b]], u_ref.at[b]) for b in range(blocks)], sems
    )
    gain_copy.wait()
    out_copies = []
    for b in range(blocks):
        u_copies[b].wait()
        inv = inverse_rms(u_ref.at[b])
        for c in range(groups):
            cols = slice(c * chans, (c + 1) * chans)
            normal = u_ref[b, :, cols].astype(F32) * inv
            out_ref[b, c] = (normal * gain_ref[:, cols]).astype(BF16)
        copy = pltpu.make_async_copy(out_ref.at[b], out_hbm.at[:, span[b]], sems.at[1 + blocks + b])
        copy.start()
        out_copies.append(copy)
    for copy in out_copies:
        copy.wait()


def norm_rows(u_rows, gain, groups):
    rows, width = u_rows.shape
    chans, blocks = width // groups, rows // ROW_BLOCK
    return call(
        norm_kernel,
        [jax.ShapeDtypeStruct((groups, rows, chans), BF16)],
        [
            pltpu.VMEM((blocks, ROW_BLOCK, width), BF16),
            pltpu.VMEM((1, width), F32),
            pltpu.VMEM((blocks, groups, ROW_BLOCK, chans), BF16),
        ],
        1 + 2 * blocks,
        "norm_rows",
        cost(8 * rows * width, 4 * rows * width),
        u_rows,
        gain,
    )[0]


def final_kernel(u_hbm, gain_hbm, grad_hbm, out_hbm, u_ref, gain_ref, grad_ref, out_ref, sems):
    blocks, groups, rows, chans = grad_ref.shape
    width = groups * chans
    span = [pl.ds(b * rows, rows) for b in range(blocks)]
    gain_copy, *copies = load(
        [(gain_hbm, gain_ref)]
        + [(u_hbm.at[span[b]], u_ref.at[b]) for b in range(blocks)]
        + [(grad_hbm.at[:, span[b]], grad_ref.at[b]) for b in range(blocks)],
        sems,
    )
    gain_copy.wait()
    out_copies = []
    for b in range(blocks):
        copies[b].wait()
        inv = inverse_rms(u_ref.at[b])
        copies[blocks + b].wait()
        total = jnp.zeros((rows, chans), F32)
        for c in range(groups):
            cols = slice(c * chans, (c + 1) * chans)
            normal = u_ref[b, :, cols].astype(F32) * inv
            total = total + normal * (gain_ref[:, cols] * grad_ref[b, c].astype(F32))
        project = jnp.sum(total, axis=1, keepdims=True) / width
        for c in range(groups):
            cols = slice(c * chans, (c + 1) * chans)
            normal = u_ref[b, :, cols].astype(F32) * inv
            scaled = gain_ref[:, cols] * grad_ref[b, c].astype(F32)
            out_ref[b, :, cols] = (inv * (scaled - normal * project)).astype(BF16)
        copy = pltpu.make_async_copy(out_ref.at[b], out_hbm.at[span[b]], sems.at[1 + 2 * blocks + b])
        copy.start()
        out_copies.append(copy)
    for copy in out_copies:
        copy.wait()


def final_rows(u_rows, gain, grad_rows):
    rows, width = u_rows.shape
    groups, _, chans = grad_rows.shape
    blocks = rows // ROW_BLOCK
    return call(
        final_kernel,
        [jax.ShapeDtypeStruct((rows, width), BF16)],
        [
            pltpu.VMEM((blocks, ROW_BLOCK, width), BF16),
            pltpu.VMEM((1, width), F32),
            pltpu.VMEM((blocks, groups, ROW_BLOCK, chans), BF16),
            pltpu.VMEM((blocks, ROW_BLOCK, width), BF16),
        ],
        1 + 3 * blocks,
        "final_rows",
        cost(16 * rows * width, 6 * rows * width),
        u_rows,
        gain,
        grad_rows,
    )[0]


def doc_starts(lens_ref):
    starts, at = [], jnp.int32(0)
    for k in range(lens_ref.shape[0] - 1):
        at = at + lens_ref[k]
        starts.append(at)
    return starts


def sort_down(codes):
    codes = list(codes)
    for end in range(len(codes) - 1, 0, -1):
        for k in range(end):
            high = jnp.maximum(codes[k], codes[k + 1])
            low = jnp.minimum(codes[k], codes[k + 1])
            codes[k], codes[k + 1] = high, low
    return codes


def cut_codes(starts, streams, base, seg_len):
    codes = []
    for start, stream in zip(starts, streams):
        place = start - base
        inside = (place >= 0) & (place < SEGS * seg_len)
        code = (place % seg_len) * 16 + place // seg_len
        codes.append(jnp.where(inside, code, 15) * 2 + stream)
    return sort_down(codes)


def any_start(starts, first, count):
    found = jnp.bool_(False)
    for start in starts:
        found = found | ((start >= first) & (start < first + count))
    return found


def time_loop(cuts_ref, seg_len, step, cut, carry):
    def piece(p, state):
        top, inner = state
        code = cuts_ref[p]
        low = code // 32
        count = top - low
        full = count // UNROLL

        def many(k, value):
            first = top - (k + 1) * UNROLL
            for j in range(UNROLL - 1, -1, -1):
                value = step(first + j, value)
            return value

        def one(k, value):
            return step(top - full * UNROLL - 1 - k, value)

        inner = lax.fori_loop(0, full, many, inner)
        inner = lax.fori_loop(0, count - full * UNROLL, one, inner)
        inner = cut((code // 2) % 16, code % 2, inner)
        return (low, inner)

    return lax.fori_loop(0, cuts_ref.shape[0], piece, (jnp.int32(seg_len), carry))[1]


def pieces(source_ref, target_ref):
    chunk = source_ref.shape[0] // PIECES
    spans = [pl.ds(k * chunk, chunk) for k in range(PIECES)]
    return [(source_ref.at[rows], target_ref.at[rows]) for rows in spans]


def widen(source_ref, target_ref, copies, chunk=32):
    halves, tokens, _ = target_ref.shape
    size = tokens // len(copies)
    for k, copy in enumerate(copies):
        copy.wait()

        def body(j, _):
            rows = pl.ds(k * size + j * chunk, chunk)
            for h in range(halves):
                target_ref[h, rows, :] = source_ref[rows, h * LANES : (h + 1) * LANES].astype(F32)
            return 0

        lax.fori_loop(0, size // chunk, body, 0)


def spread(ref, r, cols):
    return jnp.broadcast_to(ref[r : r + 1, cols], (SEGS, LANES))


def segment(ref, s, modes):
    rows = slice(s * modes, (s + 1) * modes)
    return jnp.concatenate([ref[h, rows, :] for h in range(ref.shape[0])], axis=1)


def put_segment(ref, s, modes, value):
    for h in range(ref.shape[0]):
        ref[h, s * modes : (s + 1) * modes, :] = value[:, h * LANES : (h + 1) * LANES]


def store_cuts(cuts_ref, codes):
    for k, code in enumerate(codes):
        cuts_ref[k] = code
    cuts_ref[len(codes)] = jnp.int32(30)


def leave_kernel(
    lens_hbm, rates_hbm, grad_hbm, seg_hbm, dev_hbm,
    lens_ref, rates_ref, grad_ref, seg_ref, dev_ref, wide_ref, decay_ref, cuts_ref, sems,
):
    tokens, chans = grad_ref.shape
    modes = rates_ref.shape[0]
    seg_len = tokens // SEGS
    lens_copy, rates_copy, *grad_copies = load(
        [(lens_hbm, lens_ref), (rates_hbm, rates_ref)] + pieces(grad_hbm, grad_ref), sems
    )
    base = lax.axis_index("ctx") * tokens
    lens_copy.wait()
    starts = doc_starts(lens_ref)
    store_cuts(cuts_ref, cut_codes(starts, [0] * len(starts), base, seg_len))
    rates_copy.wait()
    decay_ref[...] = jnp.exp(-rates_ref[...])
    widen(grad_ref, wide_ref, grad_copies)
    row = lax.broadcasted_iota(jnp.int32, (SEGS, LANES), 0)
    for h in range(chans // LANES):
        cols = slice(h * LANES, (h + 1) * LANES)
        decay = [spread(decay_ref, r, cols) for r in range(modes)]

        def step(i, state):
            grad = wide_ref[h, pl.ds(i, SEGS, stride=seg_len), :]
            return tuple(grad + decay[r] * state[r] for r in range(modes))

        def cut(place, stream, state):
            hold = row != place
            return tuple(jnp.where(hold, part, 0.0) for part in state)

        zero = jnp.zeros((SEGS, LANES), F32)
        state = time_loop(cuts_ref, seg_len, step, cut, (zero,) * modes)
        for r in range(modes):
            seg_ref[h, pl.ds(r, SEGS, stride=modes), :] = decay[r] * state[r]
    through = jnp.exp(-rates_ref[...] * float(seg_len))
    leaving = segment(seg_ref, SEGS - 1, modes)
    for s in range(SEGS - 2, -1, -1):
        kept = jnp.where(any_start(starts, base + s * seg_len, seg_len), 0.0, 1.0)
        leaving = segment(seg_ref, s, modes) + (through * kept) * leaving
    dev_ref[...] = leaving
    for copy in load([(dev_ref, dev_hbm), (seg_ref, seg_hbm)], sems):
        copy.wait()


def state_scratch(docs, modes, tokens, chans):
    halves = chans // LANES
    return {
        "lens": pltpu.SMEM((docs,), jnp.int32),
        "cuts": pltpu.SMEM((docs,), jnp.int32),
        "mode": pltpu.VMEM((modes, chans), F32),
        "narrow": pltpu.VMEM((tokens, chans), BF16),
        "wide": pltpu.VMEM((halves, tokens, LANES), F32),
        "segs": pltpu.VMEM((halves, SEGS * modes, LANES), F32),
    }


def leave(doc_lengths, rates, grad_out):
    modes, chans = rates.shape
    tokens = grad_out.shape[0]
    kinds = state_scratch(doc_lengths.shape[0], modes, tokens, chans)
    return call(
        leave_kernel,
        [
            jax.ShapeDtypeStruct((chans // LANES, SEGS * modes, LANES), F32),
            jax.ShapeDtypeStruct((modes, chans), F32),
        ],
        [kinds[k] for k in ("lens", "mode", "narrow", "segs", "mode", "wide", "mode", "cuts")],
        2 + PIECES,
        "leave",
        cost(2 * tokens * chans * modes, 2 * tokens * chans),
        doc_lengths,
        rates,
        grad_out,
    )


def back_kernel(
    lens_hbm, rates_hbm, residues_hbm, skip_hbm, grad_hbm, seg_hbm, *refs,
):
    later = refs[: -14]
    (out_hbm, arrive_hbm, lens_ref, rates_ref, weight_ref, skip_ref, grad_ref, seg_ref, later_ref,
     arrive_ref, wide_ref, decay_ref, cuts_ref, sems) = refs[-14:]
    tokens, chans = grad_ref.shape
    modes = rates_ref.shape[0]
    seg_len = tokens // SEGS
    lens_copy, *copies = load(
        [
            (lens_hbm, lens_ref), (rates_hbm, rates_ref), (residues_hbm, weight_ref),
            (skip_hbm, skip_ref), (seg_hbm, seg_ref),
        ]
        + [(ref, later_ref.at[k]) for k, ref in enumerate(later)]
        + pieces(grad_hbm, grad_ref),
        sems,
    )
    copies, grad_copies = copies[: 4 + len(later)], copies[4 + len(later) :]
    here = lax.axis_index("ctx")
    base = here * tokens
    lens_copy.wait()
    starts = doc_starts(lens_ref)
    store_cuts(cuts_ref, cut_codes(starts, [0] * len(starts), base, seg_len))
    for copy in copies:
        copy.wait()
    rates = rates_ref[...]
    decay_all = jnp.exp(-rates)
    decay_ref[...] = decay_all
    weight_ref[...] = weight_ref[...] * jnp.sqrt(1.0 - decay_all * decay_all)
    through = jnp.exp(-rates * float(tokens))
    arriving = jnp.zeros((modes, chans), F32)
    for k in range(len(later), 0, -1):
        kept = jnp.where(any_start(starts, (here + k) * tokens, tokens), 0.0, 1.0)
        arriving = later_ref[k - 1] + (through * kept) * arriving
    through = jnp.exp(-rates * float(seg_len))
    put_segment(arrive_ref, SEGS - 1, modes, arriving)
    for s in range(SEGS - 1, 0, -1):
        kept = jnp.where(any_start(starts, base + s * seg_len, seg_len), 0.0, 1.0)
        arriving = segment(seg_ref, s, modes) + (through * kept) * arriving
        put_segment(arrive_ref, s - 1, modes, arriving)
    arrive_copy = pltpu.make_async_copy(arrive_ref, arrive_hbm, sems.at[0])
    arrive_copy.start()
    widen(grad_ref, wide_ref, grad_copies)
    row = lax.broadcasted_iota(jnp.int32, (SEGS, LANES), 0)
    for h in range(chans // LANES):
        cols = slice(h * LANES, (h + 1) * LANES)
        decay = [spread(decay_ref, r, cols) for r in range(modes)]
        weight = [spread(weight_ref, r, cols) for r in range(modes)]
        skip = jnp.broadcast_to(skip_ref[:, cols], (SEGS, LANES))

        def step(i, state):
            rows = pl.ds(i, SEGS, stride=seg_len)
            grad = wide_ref[h, rows, :]
            back = tuple(grad + part for part in state)
            terms = [weight[r] * back[r] for r in range(modes)] + [skip * grad]
            while len(terms) > 1:
                terms = [a + b for a, b in zip(terms[::2], terms[1::2])] + terms[len(terms) // 2 * 2 :]
            wide_ref[h, rows, :] = terms[0]
            return tuple(decay[r] * back[r] for r in range(modes))

        def cut(place, stream, state):
            hold = row != place
            return tuple(jnp.where(hold, part, 0.0) for part in state)

        entry = tuple(arrive_ref[h, pl.ds(r, SEGS, stride=modes), :] for r in range(modes))
        time_loop(cuts_ref, seg_len, step, cut, entry)

    out_copies = []
    for k, (source, target) in enumerate(pieces(grad_ref, out_hbm)):
        size = target.shape[0]

        def narrow(j, _):
            rows = pl.ds(k * size + j * 32, 32)
            for h in range(wide_ref.shape[0]):
                grad_ref[rows, h * LANES : (h + 1) * LANES] = wide_ref[h, rows, :].astype(BF16)
            return 0

        lax.fori_loop(0, size // 32, narrow, 0)
        copy = pltpu.make_async_copy(source, target, sems.at[1 + k])
        copy.start()
        out_copies.append(copy)
    for copy in out_copies:
        copy.wait()
    arrive_copy.wait()


def back_pass(doc_lengths, rates, residues, skip, grad_out, seg_leaving, later):
    modes, chans = rates.shape
    tokens = grad_out.shape[0]
    kinds = state_scratch(doc_lengths.shape[0], modes, tokens, chans)
    kinds["skip"] = pltpu.VMEM((1, chans), F32)
    kinds["later"] = pltpu.VMEM((len(later), modes, chans), F32)
    names = ("lens", "mode", "mode", "skip", "narrow", "segs", "later", "segs", "wide", "mode", "cuts")
    return call(
        back_kernel,
        [
            jax.ShapeDtypeStruct((tokens, chans), BF16),
            jax.ShapeDtypeStruct((chans // LANES, SEGS * modes, LANES), F32),
        ],
        [kinds[k] for k in names],
        5 + len(later) + PIECES,
        "back_pass",
        cost(4 * tokens * chans * modes, 4 * tokens * chans),
        doc_lengths,
        rates,
        residues,
        skip,
        grad_out,
        seg_leaving,
        *later,
    )


def residue_kernel(
    window, lens_hbm, streams_hbm, rates_hbm, grad_hbm, x_hbm, arrive_hbm, out_hbm,
    lens_ref, streams_ref, rates_ref, grad_ref, x_ref, arrive_ref, out_ref,
    wide_ref, x_wide_ref, decay_ref, total_ref, cuts_ref, sems,
):
    tokens, chans = grad_ref.shape
    modes = rates_ref.shape[0]
    seg_len = tokens // SEGS
    copies = load(
        [
            (lens_hbm, lens_ref), (streams_hbm, streams_ref), (rates_hbm, rates_ref),
            (arrive_hbm, arrive_ref),
        ]
        + pieces(grad_hbm, grad_ref)
        + pieces(x_hbm, x_ref),
        sems,
    )
    base = lax.axis_index("ctx") * tokens
    for copy in copies[:4]:
        copy.wait()
    copies = copies[4:]
    starts = doc_starts(lens_ref)
    streams = [streams_ref[k] for k in range(len(starts) + 1)]
    store_cuts(cuts_ref, cut_codes(starts, streams[1:], base, seg_len))
    decay_all = jnp.exp(-rates_ref[...])
    decay_ref[...] = decay_all
    widen(grad_ref, wide_ref, copies[: len(copies) // 2])
    widen(x_ref, x_wide_ref, copies[len(copies) // 2 :])
    total_ref[...] = jnp.zeros_like(total_ref)
    row = lax.broadcasted_iota(jnp.int32, (SEGS, LANES), 0)
    first = base + row * seg_len
    stream_at = jnp.full((SEGS, LANES), streams[0], jnp.int32)
    for start, stream in zip(starts, streams[1:]):
        stream_at = jnp.where(first >= start, stream, stream_at)
    for h in range(chans // LANES):
        cols = slice(h * LANES, (h + 1) * LANES)
        decay = [spread(decay_ref, r, cols) for r in range(modes)]

        def step(i, carry):
            state, total = carry
            rows = pl.ds(i, SEGS, stride=seg_len)
            grad = wide_ref[h, rows, :]
            x = x_wide_ref[h, rows, :]
            back = tuple(grad + part for part in state)
            total = tuple(total[r] + x * back[r] for r in range(modes))
            return (tuple(decay[r] * back[r] for r in range(modes)), total)

        def cut(place, stream, carry):
            state, total = carry
            hold = row != place
            for r in range(modes):
                total_ref[stream, r, :, cols] += jnp.where(hold, 0.0, total[r])
            return (
                tuple(jnp.where(hold, part, 0.0) for part in state),
                tuple(jnp.where(hold, part, 0.0) for part in total),
            )

        zero = jnp.zeros((SEGS, LANES), F32)
        entry = tuple(arrive_ref[h, pl.ds(r, SEGS, stride=modes), :] for r in range(modes))
        _, total = time_loop(cuts_ref, seg_len, step, cut, (entry, (zero,) * modes))
        for s in range(2):
            for r in range(modes):
                total_ref[s, r, :, cols] += jnp.where(stream_at == s, total[r], 0.0)
    scale = jnp.sqrt(1.0 - decay_all * decay_all) / math.sqrt(window)
    for s in range(2):
        out_ref[s] = (jnp.sum(total_ref[s], axis=1) * scale).astype(BF16)
    for copy in load([(out_ref, out_hbm)], sems):
        copy.wait()


def residue_pass(doc_lengths, doc_streams, rates, grad_out, x_cols, arriving, window):
    modes, chans = rates.shape
    tokens = grad_out.shape[0]
    kinds = state_scratch(doc_lengths.shape[0], modes, tokens, chans)
    kinds["out"] = pltpu.VMEM((2, modes, chans), BF16)
    kinds["total"] = pltpu.VMEM((2, modes, SEGS, chans), F32)
    names = ("lens", "lens", "mode", "narrow", "narrow", "segs", "out", "wide", "wide", "mode", "total", "cuts")

    def kernel(*refs):
        residue_kernel(window, *refs)

    return call(
        kernel,
        [jax.ShapeDtypeStruct((2, modes, chans), BF16)],
        [kinds[k] for k in names],
        4 + 2 * (PIECES),
        "residue_pass",
        cost(4 * tokens * chans * modes, 4 * tokens * chans),
        doc_lengths,
        doc_streams,
        rates,
        grad_out,
        x_cols,
        arriving,
    )[0]


def from_later(value, axis):
    count = lax.axis_size(axis)
    return [
        lax.ppermute(value, axis, [(i + k, i) for i in range(count - k)]) for k in range(1, count)
    ]


def sum_over(value, axis):
    count = lax.axis_size(axis)
    parts = [value] + [
        lax.ppermute(value, axis, [(i, (i + k) % count) for i in range(count)]) for k in range(1, count)
    ]
    parts = [part.astype(F32) for part in parts]
    while len(parts) > 1:
        half = len(parts) // 2
        parts = [a + b for a, b in zip(parts[:half], parts[half:])]
    return parts[0]


def local(u_rows, gain, skip, residues, rates, grad_out, doc_lengths, doc_streams):
    ctx, groups = lax.axis_size("ctx"), lax.axis_size("ch")
    tokens, chans = grad_out.shape
    gain = gain[None, :]
    rates, residues = rates.T, residues.T
    x_send = norm_rows(u_rows, gain, groups)
    x_send, rates = lax.optimization_barrier((x_send, rates))
    x_cols = lax.all_to_all(x_send, "ch", split_axis=0, concat_axis=0, tiled=True)
    x_cols = x_cols.reshape(tokens, chans)
    seg_leaving, dev_leaving = leave(doc_lengths, rates, grad_out)
    later = from_later(dev_leaving, "ctx")
    normed_grad, arriving = back_pass(
        doc_lengths, rates, residues, skip[None, :], grad_out, seg_leaving, later
    )
    grad_rows = lax.all_to_all(
        normed_grad.reshape(groups, tokens // groups, chans), "ch", split_axis=0, concat_axis=0, tiled=True
    )
    parts = residue_pass(doc_lengths, doc_streams, rates, grad_out, x_cols, arriving, tokens * ctx)
    residue_grad = sum_over(parts, "ctx").transpose(0, 2, 1)
    input_grad = final_rows(u_rows, gain, grad_rows)
    return (input_grad, residue_grad)


def solution(mesh):
    return jax.shard_map(
        local,
        mesh=mesh,
        in_specs=(
            P(("ctx", "ch"), None),
            P(),
            P("ch"),
            P("ch", None),
            P("ch", None),
            P("ctx", "ch"),
            P(),
            P(),
        ),
        out_specs=(P(("ctx", "ch"), None), P(None, "ch", None)),
        check_vma=False,
    )
```

```python
import math

import jax
import jax.numpy as jnp
from jax import lax
from jax.experimental import pallas as pl
from jax.experimental.pallas import tpu as pltpu
from jax.sharding import PartitionSpec as P

F32 = jnp.float32
BF16 = jnp.bfloat16
SEGS = 8
LANES = 128
UNROLL = 8
PIECES = 4
CHUNK = 256
ROW_BLOCK = 16


def cost(flops, size):
    return pl.CostEstimate(flops=flops, bytes_accessed=size, transcendentals=0)


def load(pairs, sems):
    copies = [pltpu.make_async_copy(a, b, sems.at[k]) for k, (a, b) in enumerate(pairs)]
    for copy in copies:
        copy.start()
    return copies


def call(kernel, outs, scratch, sems, name, estimate, near, *operands):
    return pl.pallas_call(
        kernel,
        in_specs=[
            pl.BlockSpec(memory_space=pltpu.VMEM if k in near else pl.ANY) for k in range(len(operands))
        ],
        out_specs=[pl.BlockSpec(memory_space=pl.ANY)] * len(outs),
        out_shape=outs,
        scratch_shapes=scratch + [pltpu.SemaphoreType.DMA((sems,))],
        compiler_params=pltpu.CompilerParams(vmem_limit_bytes=60 * 1024 * 1024),
        cost_estimate=estimate,
        name=name,
    )(*operands)


def inverse_rms(u_ref, eps=1e-05):
    rows, width = u_ref.shape
    total = jnp.zeros((rows, LANES), F32)
    for c in range(width // LANES):
        part = u_ref[:, c * LANES : (c + 1) * LANES].astype(F32)
        total = total + part * part
    return lax.rsqrt(jnp.sum(total, axis=1, keepdims=True) / width + eps)


def norm_kernel(u_hbm, gain_hbm, out_hbm, u_ref, gain_ref, out_ref, sems):
    blocks, groups, rows, chans = out_ref.shape
    span = [pl.ds(b * rows, rows) for b in range(blocks)]
    gain_copy, *u_copies = load(
        [(gain_hbm, gain_ref)] + [(u_hbm.at[span[b]], u_ref.at[b]) for b in range(blocks)], sems
    )
    gain_copy.wait()
    out_copies = []
    for b in range(blocks):
        u_copies[b].wait()
        inv = inverse_rms(u_ref.at[b])
        for c in range(groups):
            cols = slice(c * chans, (c + 1) * chans)
            normal = u_ref[b, :, cols].astype(F32) * inv
            out_ref[b, c] = (normal * gain_ref[:, cols]).astype(BF16)
        copy = pltpu.make_async_copy(out_ref.at[b], out_hbm.at[:, span[b]], sems.at[1 + blocks + b])
        copy.start()
        out_copies.append(copy)
    for copy in out_copies:
        copy.wait()


def norm_rows(u_rows, gain, groups):
    rows, width = u_rows.shape
    chans, blocks = width // groups, rows // ROW_BLOCK
    return call(
        norm_kernel,
        [jax.ShapeDtypeStruct((groups, rows, chans), BF16)],
        [
            pltpu.VMEM((blocks, ROW_BLOCK, width), BF16),
            pltpu.VMEM((1, width), F32),
            pltpu.VMEM((blocks, groups, ROW_BLOCK, chans), BF16),
        ],
        1 + 2 * blocks,
        "norm_rows",
        cost(8 * rows * width, 4 * rows * width),
        (),
        u_rows,
        gain,
    )[0]


def final_kernel(u_hbm, gain_hbm, grad_ref, out_hbm, u_ref, gain_ref, out_ref, sems):
    blocks, rows, _ = u_ref.shape
    groups, _, chans = grad_ref.shape
    width = groups * chans
    span = [pl.ds(b * rows, rows) for b in range(blocks)]
    gain_copy, *copies = load(
        [(gain_hbm, gain_ref)]
        + [(u_hbm.at[span[b]], u_ref.at[b]) for b in range(blocks)],
        sems,
    )
    gain_copy.wait()
    out_copies = []
    for b in range(blocks):
        copies[b].wait()
        inv = inverse_rms(u_ref.at[b])
        total = jnp.zeros((rows, chans), F32)
        for c in range(groups):
            cols = slice(c * chans, (c + 1) * chans)
            normal = u_ref[b, :, cols].astype(F32) * inv
            total = total + normal * (gain_ref[:, cols] * grad_ref[c, span[b], :].astype(F32))
        project = jnp.sum(total, axis=1, keepdims=True) / width
        for c in range(groups):
            cols = slice(c * chans, (c + 1) * chans)
            normal = u_ref[b, :, cols].astype(F32) * inv
            scaled = gain_ref[:, cols] * grad_ref[c, span[b], :].astype(F32)
            out_ref[b, :, cols] = (inv * (scaled - normal * project)).astype(BF16)
        copy = pltpu.make_async_copy(out_ref.at[b], out_hbm.at[span[b]], sems.at[1 + blocks + b])
        copy.start()
        out_copies.append(copy)
    for copy in out_copies:
        copy.wait()


def final_rows(u_rows, gain, grad_rows):
    rows, width = u_rows.shape
    groups, _, chans = grad_rows.shape
    blocks = rows // ROW_BLOCK
    return call(
        final_kernel,
        [jax.ShapeDtypeStruct((rows, width), BF16)],
        [
            pltpu.VMEM((blocks, ROW_BLOCK, width), BF16),
            pltpu.VMEM((1, width), F32),
            pltpu.VMEM((blocks, ROW_BLOCK, width), BF16),
        ],
        1 + 2 * blocks,
        "final_rows",
        cost(16 * rows * width, 6 * rows * width),
        (2,),
        u_rows,
        gain,
        grad_rows,
    )[0]


def doc_starts(lens_ref):
    starts, at = [], jnp.int32(0)
    for k in range(lens_ref.shape[0] - 1):
        at = at + lens_ref[k]
        starts.append(at)
    return starts


def sort_down(codes):
    codes = list(codes)
    for end in range(len(codes) - 1, 0, -1):
        for k in range(end):
            high = jnp.maximum(codes[k], codes[k + 1])
            low = jnp.minimum(codes[k], codes[k + 1])
            codes[k], codes[k + 1] = high, low
    return codes


def cut_codes(starts, streams, base, seg_len):
    codes = []
    for start, stream in zip(starts, streams):
        place = start - base
        inside = (place >= 0) & (place < SEGS * seg_len)
        code = (place % seg_len) * 16 + place // seg_len
        codes.append(jnp.where(inside, code, 15) * 2 + stream)
    return sort_down(codes)


def any_start(starts, first, count):
    found = jnp.bool_(False)
    for start in starts:
        found = found | ((start >= first) & (start < first + count))
    return found


def time_loop(cuts_ref, seg_len, step, cut, carry):
    def piece(p, state):
        top, inner = state
        code = cuts_ref[p]
        low = code // 32
        count = top - low
        full = count // UNROLL

        def many(k, value):
            first = top - (k + 1) * UNROLL
            for j in range(UNROLL - 1, -1, -1):
                value = step(first + j, value)
            return value

        def one(k, value):
            return step(top - full * UNROLL - 1 - k, value)

        inner = lax.fori_loop(0, full, many, inner)
        inner = lax.fori_loop(0, count - full * UNROLL, one, inner)
        inner = cut((code // 2) % 16, code % 2, inner)
        return (low, inner)

    return lax.fori_loop(0, cuts_ref.shape[0], piece, (jnp.int32(seg_len), carry))[1]


def pieces(source_ref, target_ref):
    chunk = source_ref.shape[0] // PIECES
    spans = [pl.ds(k * chunk, chunk) for k in range(PIECES)]
    return [(source_ref.at[rows], target_ref.at[rows]) for rows in spans]


def widen(source_ref, target_ref, copies):
    halves, tokens, _ = target_ref.shape
    size = tokens // max(len(copies), 1)
    chunk = min(CHUNK, size)
    for k in range(tokens // size):
        if copies:
            copies[k].wait()

        def body(j, _):
            rows = pl.ds(k * size + j * chunk, chunk)
            for h in range(halves):
                target_ref[h, rows, :] = source_ref[rows, h * LANES : (h + 1) * LANES].astype(F32)
            return 0

        lax.fori_loop(0, size // chunk, body, 0)


def spread(ref, r, cols):
    return jnp.broadcast_to(ref[r : r + 1, cols], (SEGS, LANES))


def segment(ref, s, modes):
    rows = slice(s * modes, (s + 1) * modes)
    return jnp.concatenate([ref[h, rows, :] for h in range(ref.shape[0])], axis=1)


def put_segment(ref, s, modes, value):
    for h in range(ref.shape[0]):
        ref[h, s * modes : (s + 1) * modes, :] = value[:, h * LANES : (h + 1) * LANES]


def store_cuts(cuts_ref, codes):
    for k, code in enumerate(codes):
        cuts_ref[k] = code
    cuts_ref[len(codes)] = jnp.int32(30)


def leave_kernel(
    lens_hbm, rates_hbm, grad_hbm, seg_hbm, dev_hbm,
    lens_ref, rates_ref, grad_ref, seg_ref, dev_ref, wide_ref, decay_ref, cuts_ref, sems,
):
    tokens, chans = grad_ref.shape
    modes = rates_ref.shape[0]
    seg_len = tokens // SEGS
    lens_copy, rates_copy, *grad_copies = load(
        [(lens_hbm, lens_ref), (rates_hbm, rates_ref)] + pieces(grad_hbm, grad_ref), sems
    )
    base = lax.axis_index("ctx") * tokens
    lens_copy.wait()
    starts = doc_starts(lens_ref)
    store_cuts(cuts_ref, cut_codes(starts, [0] * len(starts), base, seg_len))
    rates_copy.wait()
    decay_ref[...] = jnp.exp(-rates_ref[...])
    widen(grad_ref, wide_ref, grad_copies)
    row = lax.broadcasted_iota(jnp.int32, (SEGS, LANES), 0)
    for h in range(chans // LANES):
        cols = slice(h * LANES, (h + 1) * LANES)
        decay = [spread(decay_ref, r, cols) for r in range(modes)]

        def step(i, state):
            grad = wide_ref[h, pl.ds(i, SEGS, stride=seg_len), :]
            return tuple(grad + decay[r] * state[r] for r in range(modes))

        def cut(place, stream, state):
            hold = row != place
            return tuple(jnp.where(hold, part, 0.0) for part in state)

        zero = jnp.zeros((SEGS, LANES), F32)
        state = time_loop(cuts_ref, seg_len, step, cut, (zero,) * modes)
        for r in range(modes):
            seg_ref[h, pl.ds(r, SEGS, stride=modes), :] = decay[r] * state[r]
    through = jnp.exp(-rates_ref[...] * float(seg_len))
    leaving = segment(seg_ref, SEGS - 1, modes)
    for s in range(SEGS - 2, -1, -1):
        kept = jnp.where(any_start(starts, base + s * seg_len, seg_len), 0.0, 1.0)
        leaving = segment(seg_ref, s, modes) + (through * kept) * leaving
    dev_ref[...] = leaving
    for copy in load([(dev_ref, dev_hbm), (seg_ref, seg_hbm)], sems):
        copy.wait()


def state_scratch(docs, modes, tokens, chans):
    halves = chans // LANES
    return {
        "lens": pltpu.SMEM((docs,), jnp.int32),
        "cuts": pltpu.SMEM((docs,), jnp.int32),
        "mode": pltpu.VMEM((modes, chans), F32),
        "narrow": pltpu.VMEM((tokens, chans), BF16),
        "wide": pltpu.VMEM((halves, tokens, LANES), F32),
        "segs": pltpu.VMEM((halves, SEGS * modes, LANES), F32),
    }


def leave(doc_lengths, rates, grad_out):
    modes, chans = rates.shape
    tokens = grad_out.shape[0]
    kinds = state_scratch(doc_lengths.shape[0], modes, tokens, chans)
    return call(
        leave_kernel,
        [
            jax.ShapeDtypeStruct((chans // LANES, SEGS * modes, LANES), F32),
            jax.ShapeDtypeStruct((modes, chans), F32),
        ],
        [kinds[k] for k in ("lens", "mode", "narrow", "segs", "mode", "wide", "mode", "cuts")],
        2 + PIECES,
        "leave",
        cost(2 * tokens * chans * modes, 2 * tokens * chans),
        (),
        doc_lengths,
        rates,
        grad_out,
    )


def back_kernel(
    lens_hbm, rates_hbm, residues_hbm, skip_hbm, grad_hbm, seg_hbm, *refs,
):
    later = refs[: -14]
    (out_hbm, arrive_hbm, lens_ref, rates_ref, weight_ref, skip_ref, grad_ref, seg_ref,
     arrive_ref, wide_ref, conv_ref, decay_ref, cuts_ref, sems) = refs[-14:]
    tokens, chans = grad_ref.shape
    modes = rates_ref.shape[0]
    seg_len = tokens // SEGS
    lens_copy, *copies = load(
        [
            (lens_hbm, lens_ref), (rates_hbm, rates_ref), (residues_hbm, weight_ref),
            (skip_hbm, skip_ref), (seg_hbm, seg_ref),
        ]
        + pieces(grad_hbm, grad_ref),
        sems,
    )
    copies, grad_copies = copies[:4], copies[4:]
    here = lax.axis_index("ctx")
    base = here * tokens
    lens_copy.wait()
    starts = doc_starts(lens_ref)
    store_cuts(cuts_ref, cut_codes(starts, [0] * len(starts), base, seg_len))
    for copy in copies:
        copy.wait()
    rates = rates_ref[...]
    decay_all = jnp.exp(-rates)
    decay_ref[...] = decay_all
    weight_ref[...] = weight_ref[...] * jnp.sqrt(1.0 - decay_all * decay_all)
    through = jnp.exp(-rates * float(tokens))
    arriving = jnp.zeros((modes, chans), F32)
    for k in range(len(later), 0, -1):
        kept = jnp.where(any_start(starts, (here + k) * tokens, tokens), 0.0, 1.0)
        arriving = later[k - 1][...] + (through * kept) * arriving
    through = jnp.exp(-rates * float(seg_len))
    put_segment(arrive_ref, SEGS - 1, modes, arriving)
    for s in range(SEGS - 1, 0, -1):
        kept = jnp.where(any_start(starts, base + s * seg_len, seg_len), 0.0, 1.0)
        arriving = segment(seg_ref, s, modes) + (through * kept) * arriving
        put_segment(arrive_ref, s - 1, modes, arriving)
    arrive_copy = pltpu.make_async_copy(arrive_ref, arrive_hbm, sems.at[0])
    arrive_copy.start()
    widen(grad_ref, wide_ref, grad_copies)
    row = lax.broadcasted_iota(jnp.int32, (SEGS, LANES), 0)
    for h in range(chans // LANES):
        cols = slice(h * LANES, (h + 1) * LANES)
        decay = [spread(decay_ref, r, cols) for r in range(modes)]
        weight = [spread(weight_ref, r, cols) for r in range(modes)]
        skip = jnp.broadcast_to(skip_ref[:, cols], (SEGS, LANES))

        def step(i, state):
            rows = pl.ds(i, SEGS, stride=seg_len)
            grad = wide_ref[h, rows, :]
            back = tuple(grad + part for part in state)
            terms = [weight[r] * back[r] for r in range(modes)] + [skip * grad]
            while len(terms) > 1:
                terms = [a + b for a, b in zip(terms[::2], terms[1::2])] + terms[len(terms) // 2 * 2 :]
            conv_ref[h, rows, :] = terms[0]
            return tuple(decay[r] * back[r] for r in range(modes))

        def cut(place, stream, state):
            hold = row != place
            return tuple(jnp.where(hold, part, 0.0) for part in state)

        entry = tuple(arrive_ref[h, pl.ds(r, SEGS, stride=modes), :] for r in range(modes))
        time_loop(cuts_ref, seg_len, step, cut, entry)

    out_copies = []
    for k, (source, target) in enumerate(pieces(grad_ref, out_hbm)):
        size = target.shape[0]
        chunk = min(CHUNK, size)

        def narrow(j, _):
            rows = pl.ds(k * size + j * chunk, chunk)
            for h in range(conv_ref.shape[0]):
                grad_ref[rows, h * LANES : (h + 1) * LANES] = conv_ref[h, rows, :].astype(BF16)
            return 0

        lax.fori_loop(0, size // chunk, narrow, 0)
        copy = pltpu.make_async_copy(source, target, sems.at[1 + k])
        copy.start()
        out_copies.append(copy)
    for copy in out_copies:
        copy.wait()
    arrive_copy.wait()


def back_pass(doc_lengths, rates, residues, skip, grad_out, seg_leaving, later):
    modes, chans = rates.shape
    tokens = grad_out.shape[0]
    kinds = state_scratch(doc_lengths.shape[0], modes, tokens, chans)
    kinds["skip"] = pltpu.VMEM((1, chans), F32)
    names = ("lens", "mode", "mode", "skip", "narrow", "segs", "segs", "wide", "wide", "mode", "cuts")
    return call(
        back_kernel,
        [
            jax.ShapeDtypeStruct((tokens, chans), BF16),
            jax.ShapeDtypeStruct((chans // LANES, SEGS * modes, LANES), F32),
        ],
        [kinds[k] for k in names],
        5 + PIECES,
        "back_pass",
        cost(4 * tokens * chans * modes, 4 * tokens * chans),
        range(6, 6 + len(later)),
        doc_lengths,
        rates,
        residues,
        skip,
        grad_out,
        seg_leaving,
        *later,
    )


def residue_kernel(
    window, lens_hbm, streams_hbm, rates_hbm, grad_hbm, x_ref, arrive_hbm, out_hbm,
    lens_ref, streams_ref, rates_ref, grad_ref, arrive_ref, out_ref,
    wide_ref, x_wide_ref, decay_ref, total_ref, cuts_ref, sems,
):
    tokens, chans = grad_ref.shape
    modes = rates_ref.shape[0]
    seg_len = tokens // SEGS
    copies = load(
        [
            (lens_hbm, lens_ref), (streams_hbm, streams_ref), (rates_hbm, rates_ref),
            (arrive_hbm, arrive_ref),
        ]
        + pieces(grad_hbm, grad_ref),
        sems,
    )
    base = lax.axis_index("ctx") * tokens
    for copy in copies[:4]:
        copy.wait()
    copies = copies[4:]
    starts = doc_starts(lens_ref)
    streams = [streams_ref[k] for k in range(len(starts) + 1)]
    store_cuts(cuts_ref, cut_codes(starts, streams[1:], base, seg_len))
    decay_all = jnp.exp(-rates_ref[...])
    decay_ref[...] = decay_all
    widen(x_ref, x_wide_ref, ())
    widen(grad_ref, wide_ref, copies)
    total_ref[...] = jnp.zeros_like(total_ref)
    row = lax.broadcasted_iota(jnp.int32, (SEGS, LANES), 0)
    first = base + row * seg_len
    stream_at = jnp.full((SEGS, LANES), streams[0], jnp.int32)
    for start, stream in zip(starts, streams[1:]):
        stream_at = jnp.where(first >= start, stream, stream_at)
    for h in range(chans // LANES):
        cols = slice(h * LANES, (h + 1) * LANES)
        decay = [spread(decay_ref, r, cols) for r in range(modes)]

        def step(i, carry):
            state, total = carry
            rows = pl.ds(i, SEGS, stride=seg_len)
            grad = wide_ref[h, rows, :]
            x = x_wide_ref[h, rows, :]
            back = tuple(grad + part for part in state)
            total = tuple(total[r] + x * back[r] for r in range(modes))
            return (tuple(decay[r] * back[r] for r in range(modes)), total)

        def cut(place, stream, carry):
            state, total = carry
            hold = row != place
            for r in range(modes):
                total_ref[stream, r, :, cols] += jnp.where(hold, 0.0, total[r])
            return (
                tuple(jnp.where(hold, part, 0.0) for part in state),
                tuple(jnp.where(hold, part, 0.0) for part in total),
            )

        zero = jnp.zeros((SEGS, LANES), F32)
        entry = tuple(arrive_ref[h, pl.ds(r, SEGS, stride=modes), :] for r in range(modes))
        _, total = time_loop(cuts_ref, seg_len, step, cut, (entry, (zero,) * modes))
        for s in range(2):
            for r in range(modes):
                total_ref[s, r, :, cols] += jnp.where(stream_at == s, total[r], 0.0)
    scale = jnp.sqrt(1.0 - decay_all * decay_all) / math.sqrt(window)
    for s in range(2):
        out_ref[s] = (jnp.sum(total_ref[s], axis=1) * scale).astype(BF16)
    for copy in load([(out_ref, out_hbm)], sems):
        copy.wait()


def residue_pass(doc_lengths, doc_streams, rates, grad_out, x_cols, arriving, window):
    modes, chans = rates.shape
    tokens = grad_out.shape[0]
    kinds = state_scratch(doc_lengths.shape[0], modes, tokens, chans)
    kinds["out"] = pltpu.VMEM((2, modes, chans), BF16)
    kinds["total"] = pltpu.VMEM((2, modes, SEGS, chans), F32)
    names = ("lens", "lens", "mode", "narrow", "segs", "out", "wide", "wide", "mode", "total", "cuts")

    def kernel(*refs):
        residue_kernel(window, *refs)

    return call(
        kernel,
        [jax.ShapeDtypeStruct((2, modes, chans), BF16)],
        [kinds[k] for k in names],
        4 + PIECES,
        "residue_pass",
        cost(4 * tokens * chans * modes, 4 * tokens * chans),
        (4,),
        doc_lengths,
        doc_streams,
        rates,
        grad_out,
        x_cols,
        arriving,
    )[0]


def from_later(value, axis):
    count = lax.axis_size(axis)
    return [
        lax.ppermute(value, axis, [(i + k, i) for i in range(count - k)])
        for k in range(1, max(2, count // 2 + 1))
    ]


def sum_over(value, axis):
    count = lax.axis_size(axis)
    half = count // 2
    parts = [value] + [
        lax.ppermute(value, axis, [(i, i // half * half + (i + k) % half) for i in range(count)])
        for k in range(1, half)
    ]
    parts = [part.astype(F32) for part in parts]
    while len(parts) > 1:
        middle = len(parts) // 2
        parts = [a + b for a, b in zip(parts[:middle], parts[middle:])]
    other = lax.ppermute(parts[0], axis, [(i, (i + half) % count) for i in range(count)])
    return parts[0] + other


def local(u_rows, gain, skip, residues, rates, grad_out, doc_lengths, doc_streams):
    ctx, groups = lax.axis_size("ctx"), lax.axis_size("ch")
    tokens, chans = grad_out.shape
    gain = gain[None, :]
    rates, residues = rates.T, residues.T
    x_send = norm_rows(u_rows, gain, groups)
    x_send, rates = lax.optimization_barrier((x_send, rates))
    x_cols = lax.all_to_all(x_send, "ch", split_axis=0, concat_axis=0, tiled=True)
    x_cols = x_cols.reshape(tokens, chans)
    seg_leaving, dev_leaving = leave(doc_lengths, rates, grad_out)
    later = from_later(dev_leaving, "ctx")
    normed_grad, arriving = back_pass(
        doc_lengths, rates, residues, skip[None, :], grad_out, seg_leaving, later
    )
    grad_rows = lax.all_to_all(
        normed_grad.reshape(groups, tokens // groups, chans), "ch", split_axis=0, concat_axis=0, tiled=True
    )
    parts = residue_pass(doc_lengths, doc_streams, rates, grad_out, x_cols, arriving, tokens * ctx)
    residue_grad = sum_over(parts, "ctx").transpose(0, 2, 1)
    input_grad = final_rows(u_rows, gain, grad_rows)
    return (input_grad, residue_grad)


def solution(mesh):
    return jax.shard_map(
        local,
        mesh=mesh,
        in_specs=(
            P(("ctx", "ch"), None),
            P(),
            P("ch"),
            P("ch", None),
            P("ch", None),
            P("ctx", "ch"),
            P(),
            P(),
        ),
        out_specs=(P(("ctx", "ch"), None), P(None, "ch", None)),
        check_vma=False,
    )
```

```python
import math

import jax
import jax.numpy as jnp
from jax import lax
from jax.experimental import pallas as pl
from jax.experimental.pallas import tpu as pltpu
from jax.sharding import PartitionSpec as P

F32 = jnp.float32
BF16 = jnp.bfloat16
SEGS = 8
LANES = 128
UNROLL = 8
PIECES = 4
CHUNK = 256
ROW_BLOCK = 16


def cost(flops, size):
    return pl.CostEstimate(flops=flops, bytes_accessed=size, transcendentals=0)


def load(pairs, sems):
    copies = [pltpu.make_async_copy(a, b, sems.at[k]) for k, (a, b) in enumerate(pairs)]
    for copy in copies:
        copy.start()
    return copies


def call(kernel, outs, scratch, sems, name, estimate, near, *operands):
    return pl.pallas_call(
        kernel,
        in_specs=[
            pl.BlockSpec(memory_space=pltpu.VMEM if k in near else pltpu.HBM) for k in range(len(operands))
        ],
        out_specs=[pl.BlockSpec(memory_space=pltpu.HBM)] * len(outs),
        out_shape=outs,
        scratch_shapes=scratch + [pltpu.SemaphoreType.DMA((sems,))],
        compiler_params=pltpu.CompilerParams(vmem_limit_bytes=16 * 1024 * 1024),
        cost_estimate=estimate,
        name=name,
    )(*operands)


def inverse_rms(u_ref, eps=1e-05):
    rows, width = u_ref.shape
    total = jnp.zeros((rows, LANES), F32)
    for c in range(width // LANES):
        part = u_ref[:, c * LANES : (c + 1) * LANES].astype(F32)
        total = total + part * part
    return lax.rsqrt(jnp.sum(total, axis=1, keepdims=True) / width + eps)


def norm_kernel(u_hbm, gain_hbm, out_hbm, u_ref, gain_ref, out_ref, sems):
    blocks, groups, rows, chans = out_ref.shape
    span = [pl.ds(b * rows, rows) for b in range(blocks)]
    gain_copy, *u_copies = load(
        [(gain_hbm, gain_ref)] + [(u_hbm.at[span[b]], u_ref.at[b]) for b in range(blocks)], sems
    )
    gain_copy.wait()
    out_copies = []
    for b in range(blocks):
        u_copies[b].wait()
        inv = inverse_rms(u_ref.at[b])
        for c in range(groups):
            cols = slice(c * chans, (c + 1) * chans)
            normal = u_ref[b, :, cols].astype(F32) * inv
            out_ref[b, c] = (normal * gain_ref[:, cols]).astype(BF16)
        copy = pltpu.make_async_copy(out_ref.at[b], out_hbm.at[:, span[b]], sems.at[1 + blocks + b])
        copy.start()
        out_copies.append(copy)
    for copy in out_copies:
        copy.wait()


def norm_rows(u_rows, gain, groups):
    rows, width = u_rows.shape
    chans, blocks = width // groups, rows // ROW_BLOCK
    return call(
        norm_kernel,
        [jax.ShapeDtypeStruct((groups, rows, chans), BF16)],
        [
            pltpu.VMEM((blocks, ROW_BLOCK, width), BF16),
            pltpu.VMEM((1, width), F32),
            pltpu.VMEM((blocks, groups, ROW_BLOCK, chans), BF16),
        ],
        1 + 2 * blocks,
        "norm_rows",
        cost(8 * rows * width, 4 * rows * width),
        (),
        u_rows,
        gain,
    )[0]


def final_kernel(u_hbm, gain_hbm, grad_ref, out_hbm, u_ref, gain_ref, out_ref, sems):
    blocks, rows, _ = u_ref.shape
    groups, _, chans = grad_ref.shape
    width = groups * chans
    span = [pl.ds(b * rows, rows) for b in range(blocks)]
    gain_copy, *copies = load(
        [(gain_hbm, gain_ref)]
        + [(u_hbm.at[span[b]], u_ref.at[b]) for b in range(blocks)],
        sems,
    )
    gain_copy.wait()
    out_copies = []
    for b in range(blocks):
        copies[b].wait()
        inv = inverse_rms(u_ref.at[b])
        total = jnp.zeros((rows, chans), F32)
        for c in range(groups):
            cols = slice(c * chans, (c + 1) * chans)
            normal = u_ref[b, :, cols].astype(F32) * inv
            total = total + normal * (gain_ref[:, cols] * grad_ref[c, span[b], :].astype(F32))
        project = jnp.sum(total, axis=1, keepdims=True) / width
        for c in range(groups):
            cols = slice(c * chans, (c + 1) * chans)
            normal = u_ref[b, :, cols].astype(F32) * inv
            scaled = gain_ref[:, cols] * grad_ref[c, span[b], :].astype(F32)
            out_ref[b, :, cols] = (inv * (scaled - normal * project)).astype(BF16)
        copy = pltpu.make_async_copy(out_ref.at[b], out_hbm.at[span[b]], sems.at[1 + blocks + b])
        copy.start()
        out_copies.append(copy)
    for copy in out_copies:
        copy.wait()


def final_rows(u_rows, gain, grad_rows):
    rows, width = u_rows.shape
    groups, _, chans = grad_rows.shape
    blocks = rows // ROW_BLOCK
    return call(
        final_kernel,
        [jax.ShapeDtypeStruct((rows, width), BF16)],
        [
            pltpu.VMEM((blocks, ROW_BLOCK, width), BF16),
            pltpu.VMEM((1, width), F32),
            pltpu.VMEM((blocks, ROW_BLOCK, width), BF16),
        ],
        1 + 2 * blocks,
        "final_rows",
        cost(16 * rows * width, 6 * rows * width),
        (2,),
        u_rows,
        gain,
        grad_rows,
    )[0]


def doc_starts(lens_ref):
    starts, at = [], jnp.int32(0)
    for k in range(lens_ref.shape[0] - 1):
        at = at + lens_ref[k]
        starts.append(at)
    return starts


def sort_down(codes):
    codes = list(codes)
    for end in range(len(codes) - 1, 0, -1):
        for k in range(end):
            high = jnp.maximum(codes[k], codes[k + 1])
            low = jnp.minimum(codes[k], codes[k + 1])
            codes[k], codes[k + 1] = high, low
    return codes


def cut_codes(starts, streams, base, seg_len):
    codes = []
    for start, stream in zip(starts, streams):
        place = start - base
        inside = (place >= 0) & (place < SEGS * seg_len)
        code = (place % seg_len) * 16 + place // seg_len
        codes.append(jnp.where(inside, code, 15) * 2 + stream)
    return sort_down(codes)


def any_start(starts, first, count):
    found = jnp.bool_(False)
    for start in starts:
        found = found | ((start >= first) & (start < first + count))
    return found


def time_loop(cuts_ref, seg_len, step, cut, carry):
    def piece(p, state):
        top, inner = state
        code = cuts_ref[p]
        low = code // 32
        count = top - low
        full = count // UNROLL

        def many(k, value):
            first = top - (k + 1) * UNROLL
            for j in range(UNROLL - 1, -1, -1):
                value = step(first + j, value)
            return value

        def one(k, value):
            return step(top - full * UNROLL - 1 - k, value)

        inner = lax.fori_loop(0, full, many, inner)
        inner = lax.fori_loop(0, count - full * UNROLL, one, inner)
        inner = cut((code // 2) % 16, code % 2, inner)
        return (low, inner)

    return lax.fori_loop(0, cuts_ref.shape[0], piece, (jnp.int32(seg_len), carry))[1]


def pieces(source_ref, target_ref):
    chunk = source_ref.shape[0] // PIECES
    spans = [pl.ds(k * chunk, chunk) for k in range(PIECES)]
    return [(source_ref.at[rows], target_ref.at[rows]) for rows in spans]


def widen(source_ref, target_ref, copies):
    halves, tokens, _ = target_ref.shape
    size = tokens // max(len(copies), 1)
    chunk = min(CHUNK, size)
    for k in range(tokens // size):
        if copies:
            copies[k].wait()

        def body(j, _):
            rows = pl.ds(k * size + j * chunk, chunk)
            for h in range(halves):
                target_ref[h, rows, :] = source_ref[rows, h * LANES : (h + 1) * LANES].astype(F32)
            return 0

        lax.fori_loop(0, size // chunk, body, 0)


def spread(ref, r, cols):
    return jnp.broadcast_to(ref[r : r + 1, cols], (SEGS, LANES))


def segment(ref, s, modes):
    rows = slice(s * modes, (s + 1) * modes)
    return jnp.concatenate([ref[h, rows, :] for h in range(ref.shape[0])], axis=1)


def put_segment(ref, s, modes, value):
    for h in range(ref.shape[0]):
        ref[h, s * modes : (s + 1) * modes, :] = value[:, h * LANES : (h + 1) * LANES]


def store_cuts(cuts_ref, codes):
    for k, code in enumerate(codes):
        cuts_ref[k] = code
    cuts_ref[len(codes)] = jnp.int32(30)


def leave_kernel(
    lens_hbm, rates_hbm, grad_hbm, seg_hbm, dev_hbm,
    lens_ref, rates_ref, grad_ref, seg_ref, dev_ref, wide_ref, decay_ref, cuts_ref, sems,
):
    tokens, chans = grad_ref.shape
    modes = rates_ref.shape[0]
    seg_len = tokens // SEGS
    lens_copy, rates_copy, *grad_copies = load(
        [(lens_hbm, lens_ref), (rates_hbm, rates_ref)] + pieces(grad_hbm, grad_ref), sems
    )
    base = lax.axis_index("ctx") * tokens
    lens_copy.wait()
    starts = doc_starts(lens_ref)
    store_cuts(cuts_ref, cut_codes(starts, [0] * len(starts), base, seg_len))
    rates_copy.wait()
    decay_ref[...] = jnp.exp(-rates_ref[...])
    widen(grad_ref, wide_ref, grad_copies)
    row = lax.broadcasted_iota(jnp.int32, (SEGS, LANES), 0)
    for h in range(chans // LANES):
        cols = slice(h * LANES, (h + 1) * LANES)
        decay = [spread(decay_ref, r, cols) for r in range(modes)]

        def step(i, state):
            grad = wide_ref[h, pl.ds(i, SEGS, stride=seg_len), :]
            return tuple(grad + decay[r] * state[r] for r in range(modes))

        def cut(place, stream, state):
            hold = row != place
            return tuple(jnp.where(hold, part, 0.0) for part in state)

        zero = jnp.zeros((SEGS, LANES), F32)
        state = time_loop(cuts_ref, seg_len, step, cut, (zero,) * modes)
        for r in range(modes):
            seg_ref[h, pl.ds(r, SEGS, stride=modes), :] = decay[r] * state[r]
    through = jnp.exp(-rates_ref[...] * float(seg_len))
    leaving = segment(seg_ref, SEGS - 1, modes)
    for s in range(SEGS - 2, -1, -1):
        kept = jnp.where(any_start(starts, base + s * seg_len, seg_len), 0.0, 1.0)
        leaving = segment(seg_ref, s, modes) + (through * kept) * leaving
    dev_ref[...] = leaving
    for copy in load([(dev_ref, dev_hbm), (seg_ref, seg_hbm)], sems):
        copy.wait()


def state_scratch(docs, modes, tokens, chans):
    halves = chans // LANES
    return {
        "lens": pltpu.SMEM((docs,), jnp.int32),
        "cuts": pltpu.SMEM((docs,), jnp.int32),
        "mode": pltpu.VMEM((modes, chans), F32),
        "narrow": pltpu.VMEM((tokens, chans), BF16),
        "wide": pltpu.VMEM((halves, tokens, LANES), F32),
        "segs": pltpu.VMEM((halves, SEGS * modes, LANES), F32),
    }


def leave(doc_lengths, rates, grad_out):
    modes, chans = rates.shape
    tokens = grad_out.shape[0]
    kinds = state_scratch(doc_lengths.shape[0], modes, tokens, chans)
    return call(
        leave_kernel,
        [
            jax.ShapeDtypeStruct((chans // LANES, SEGS * modes, LANES), F32),
            jax.ShapeDtypeStruct((modes, chans), F32),
        ],
        [kinds[k] for k in ("lens", "mode", "narrow", "segs", "mode", "wide", "mode", "cuts")],
        2 + PIECES,
        "leave",
        cost(2 * tokens * chans * modes, 2 * tokens * chans),
        (),
        doc_lengths,
        rates,
        grad_out,
    )


def back_kernel(
    lens_hbm, rates_hbm, residues_hbm, skip_hbm, grad_hbm, seg_hbm, *refs,
):
    later = refs[: -14]
    (out_hbm, arrive_hbm, lens_ref, rates_ref, weight_ref, skip_ref, grad_ref, seg_ref,
     arrive_ref, wide_ref, conv_ref, decay_ref, cuts_ref, sems) = refs[-14:]
    tokens, chans = grad_ref.shape
    modes = rates_ref.shape[0]
    seg_len = tokens // SEGS
    lens_copy, *copies = load(
        [
            (lens_hbm, lens_ref), (rates_hbm, rates_ref), (residues_hbm, weight_ref),
            (skip_hbm, skip_ref), (seg_hbm, seg_ref),
        ]
        + pieces(grad_hbm, grad_ref),
        sems,
    )
    copies, grad_copies = copies[:4], copies[4:]
    here, last = lax.axis_index("ctx"), lax.axis_size("ctx")
    base = here * tokens
    lens_copy.wait()
    starts = doc_starts(lens_ref)
    store_cuts(cuts_ref, cut_codes(starts, [0] * len(starts), base, seg_len))
    for copy in copies:
        copy.wait()
    rates = rates_ref[...]
    decay_all = jnp.exp(-rates)
    decay_ref[...] = decay_all
    weight_ref[...] = weight_ref[...] * jnp.sqrt(1.0 - decay_all * decay_all)
    through = jnp.exp(-rates * float(tokens))
    arriving = jnp.zeros((modes, chans), F32)
    for k in range(len(later), 0, -1):
        kept = jnp.where(any_start(starts, (here + k) * tokens, tokens), 0.0, 1.0)
        arriving = later[k - 1][...] + (through * kept) * arriving
        arriving = jnp.where(here + k < last, arriving, 0.0)
    through = jnp.exp(-rates * float(seg_len))
    put_segment(arrive_ref, SEGS - 1, modes, arriving)
    for s in range(SEGS - 1, 0, -1):
        kept = jnp.where(any_start(starts, base + s * seg_len, seg_len), 0.0, 1.0)
        arriving = segment(seg_ref, s, modes) + (through * kept) * arriving
        put_segment(arrive_ref, s - 1, modes, arriving)
    arrive_copy = pltpu.make_async_copy(arrive_ref, arrive_hbm, sems.at[0])
    arrive_copy.start()
    widen(grad_ref, wide_ref, grad_copies)
    row = lax.broadcasted_iota(jnp.int32, (SEGS, LANES), 0)
    for h in range(chans // LANES):
        cols = slice(h * LANES, (h + 1) * LANES)
        decay = [spread(decay_ref, r, cols) for r in range(modes)]
        weight = [spread(weight_ref, r, cols) for r in range(modes)]
        skip = jnp.broadcast_to(skip_ref[:, cols], (SEGS, LANES))

        def step(i, state):
            rows = pl.ds(i, SEGS, stride=seg_len)
            grad = wide_ref[h, rows, :]
            back = tuple(grad + part for part in state)
            terms = [weight[r] * back[r] for r in range(modes)] + [skip * grad]
            while len(terms) > 1:
                terms = [a + b for a, b in zip(terms[::2], terms[1::2])] + terms[len(terms) // 2 * 2 :]
            conv_ref[h, rows, :] = terms[0]
            return tuple(decay[r] * back[r] for r in range(modes))

        def cut(place, stream, state):
            hold = row != place
            return tuple(jnp.where(hold, part, 0.0) for part in state)

        entry = tuple(arrive_ref[h, pl.ds(r, SEGS, stride=modes), :] for r in range(modes))
        time_loop(cuts_ref, seg_len, step, cut, entry)

    out_copies = []
    for k, (source, target) in enumerate(pieces(grad_ref, out_hbm)):
        size = target.shape[0]
        chunk = min(CHUNK, size)

        def narrow(j, _):
            rows = pl.ds(k * size + j * chunk, chunk)
            for h in range(conv_ref.shape[0]):
                grad_ref[rows, h * LANES : (h + 1) * LANES] = conv_ref[h, rows, :].astype(BF16)
            return 0

        lax.fori_loop(0, size // chunk, narrow, 0)
        copy = pltpu.make_async_copy(source, target, sems.at[1 + k])
        copy.start()
        out_copies.append(copy)
    for copy in out_copies:
        copy.wait()
    arrive_copy.wait()


def back_pass(doc_lengths, rates, residues, skip, grad_out, seg_leaving, later):
    modes, chans = rates.shape
    tokens = grad_out.shape[0]
    kinds = state_scratch(doc_lengths.shape[0], modes, tokens, chans)
    kinds["skip"] = pltpu.VMEM((1, chans), F32)
    names = ("lens", "mode", "mode", "skip", "narrow", "segs", "segs", "wide", "wide", "mode", "cuts")
    return call(
        back_kernel,
        [
            jax.ShapeDtypeStruct((tokens, chans), BF16),
            jax.ShapeDtypeStruct((chans // LANES, SEGS * modes, LANES), F32),
        ],
        [kinds[k] for k in names],
        5 + PIECES,
        "back_pass",
        cost(4 * tokens * chans * modes, 4 * tokens * chans),
        range(6, 6 + len(later)),
        doc_lengths,
        rates,
        residues,
        skip,
        grad_out,
        seg_leaving,
        *later,
    )


def residue_kernel(
    window, lens_hbm, streams_hbm, rates_hbm, grad_hbm, x_ref, arrive_hbm, out_hbm,
    lens_ref, streams_ref, rates_ref, grad_ref, arrive_ref, out_ref,
    wide_ref, x_wide_ref, decay_ref, total_ref, cuts_ref, sems,
):
    tokens, chans = grad_ref.shape
    modes = rates_ref.shape[0]
    seg_len = tokens // SEGS
    copies = load(
        [
            (lens_hbm, lens_ref), (streams_hbm, streams_ref), (rates_hbm, rates_ref),
            (arrive_hbm, arrive_ref),
        ]
        + pieces(grad_hbm, grad_ref),
        sems,
    )
    base = lax.axis_index("ctx") * tokens
    for copy in copies[:4]:
        copy.wait()
    copies = copies[4:]
    starts = doc_starts(lens_ref)
    streams = [streams_ref[k] for k in range(len(starts) + 1)]
    store_cuts(cuts_ref, cut_codes(starts, streams[1:], base, seg_len))
    decay_all = jnp.exp(-rates_ref[...])
    decay_ref[...] = decay_all
    widen(x_ref, x_wide_ref, ())
    widen(grad_ref, wide_ref, copies)
    total_ref[...] = jnp.zeros_like(total_ref)
    row = lax.broadcasted_iota(jnp.int32, (SEGS, LANES), 0)
    first = base + row * seg_len
    stream_at = jnp.full((SEGS, LANES), streams[0], jnp.int32)
    for start, stream in zip(starts, streams[1:]):
        stream_at = jnp.where(first >= start, stream, stream_at)
    for h in range(chans // LANES):
        cols = slice(h * LANES, (h + 1) * LANES)
        decay = [spread(decay_ref, r, cols) for r in range(modes)]

        def step(i, carry):
            state, total = carry
            rows = pl.ds(i, SEGS, stride=seg_len)
            grad = wide_ref[h, rows, :]
            x = x_wide_ref[h, rows, :]
            back = tuple(grad + part for part in state)
            total = tuple(total[r] + x * back[r] for r in range(modes))
            return (tuple(decay[r] * back[r] for r in range(modes)), total)

        def cut(place, stream, carry):
            state, total = carry
            hold = row != place
            for r in range(modes):
                total_ref[stream, r, :, cols] += jnp.where(hold, 0.0, total[r])
            return (
                tuple(jnp.where(hold, part, 0.0) for part in state),
                tuple(jnp.where(hold, part, 0.0) for part in total),
            )

        zero = jnp.zeros((SEGS, LANES), F32)
        entry = tuple(arrive_ref[h, pl.ds(r, SEGS, stride=modes), :] for r in range(modes))
        _, total = time_loop(cuts_ref, seg_len, step, cut, (entry, (zero,) * modes))
        for s in range(2):
            for r in range(modes):
                total_ref[s, r, :, cols] += jnp.where(stream_at == s, total[r], 0.0)
    scale = jnp.sqrt(1.0 - decay_all * decay_all) / math.sqrt(window)
    for s in range(2):
        out_ref[s] = (jnp.sum(total_ref[s], axis=1) * scale).astype(BF16)
    for copy in load([(out_ref, out_hbm)], sems):
        copy.wait()


def residue_pass(doc_lengths, doc_streams, rates, grad_out, x_cols, arriving, window):
    modes, chans = rates.shape
    tokens = grad_out.shape[0]
    kinds = state_scratch(doc_lengths.shape[0], modes, tokens, chans)
    kinds["out"] = pltpu.VMEM((2, modes, chans), BF16)
    kinds["total"] = pltpu.VMEM((2, modes, SEGS, chans), F32)
    names = ("lens", "lens", "mode", "narrow", "segs", "out", "wide", "wide", "mode", "total", "cuts")

    def kernel(*refs):
        residue_kernel(window, *refs)

    return call(
        kernel,
        [jax.ShapeDtypeStruct((2, modes, chans), BF16)],
        [kinds[k] for k in names],
        4 + PIECES,
        "residue_pass",
        cost(4 * tokens * chans * modes, 4 * tokens * chans),
        (4,),
        doc_lengths,
        doc_streams,
        rates,
        grad_out,
        x_cols,
        arriving,
    )[0]


def from_later(value, axis):
    count = lax.axis_size(axis)
    return [
        lax.ppermute(value, axis, [((i + k) % count, i) for i in range(count)])
        for k in range(1, count // 2 + 1)
    ]


def sum_over(value, axis):
    count = lax.axis_size(axis)
    half = count // 2
    parts = [value] + [
        lax.ppermute(value, axis, [(i, i // half * half + (i + k) % half) for i in range(count)])
        for k in range(1, half)
    ]
    parts = [part.astype(F32) for part in parts]
    while len(parts) > 1:
        middle = len(parts) // 2
        parts = [a + b for a, b in zip(parts[:middle], parts[middle:])]
    other = lax.ppermute(parts[0], axis, [(i, (i + half) % count) for i in range(count)])
    return parts[0] + other


def local(u_rows, gain, skip, residues, rates, grad_out, doc_lengths, doc_streams):
    ctx, groups = lax.axis_size("ctx"), lax.axis_size("ch")
    tokens, chans = grad_out.shape
    gain = gain[None, :]
    rates, residues = rates.T, residues.T
    x_send = norm_rows(u_rows, gain, groups)
    x_send, rates = lax.optimization_barrier((x_send, rates))
    x_cols = lax.all_to_all(x_send, "ch", split_axis=0, concat_axis=0, tiled=True)
    x_cols = x_cols.reshape(tokens, chans)
    seg_leaving, dev_leaving = leave(doc_lengths, rates, grad_out)
    later = from_later(dev_leaving, "ctx")
    normed_grad, arriving = back_pass(
        doc_lengths, rates, residues, skip[None, :], grad_out, seg_leaving, later
    )
    grad_rows = lax.all_to_all(
        normed_grad.reshape(groups, tokens // groups, chans), "ch", split_axis=0, concat_axis=0, tiled=True
    )
    parts = residue_pass(doc_lengths, doc_streams, rates, grad_out, x_cols, arriving, tokens * ctx)
    residue_grad = sum_over(parts, "ctx").transpose(0, 2, 1)
    input_grad = final_rows(u_rows, gain, grad_rows)
    return (input_grad, residue_grad)


def solution(mesh):
    return jax.shard_map(
        local,
        mesh=mesh,
        in_specs=(
            P(("ctx", "ch"), None),
            P(),
            P("ch"),
            P("ch", None),
            P("ch", None),
            P("ctx", "ch"),
            P(),
            P(),
        ),
        out_specs=(P(("ctx", "ch"), None), P(None, "ch", None)),
        check_vma=False,
    )
```

```python
import math

import jax
import jax.numpy as jnp
from jax import lax
from jax.experimental import pallas as pl
from jax.experimental.pallas import tpu as pltpu
from jax.sharding import PartitionSpec as P

F32 = jnp.float32
BF16 = jnp.bfloat16
SEGS = 8
LANES = 128
UNROLL = 8
STEPS = 32
ROW_BLOCK = 16


def cost(flops, size):
    return pl.CostEstimate(flops=flops, bytes_accessed=size, transcendentals=0)


def load(pairs, sems):
    copies = [pltpu.make_async_copy(a, b, sems.at[k]) for k, (a, b) in enumerate(pairs)]
    for copy in copies:
        copy.start()
    return copies


def call(kernel, outs, scratch, name, estimate, spaces, out_spaces, operands, limit=16):
    return pl.pallas_call(
        kernel,
        in_specs=[pl.BlockSpec(memory_space=space) for space in spaces],
        out_specs=[pl.BlockSpec(memory_space=space) for space in out_spaces],
        out_shape=outs,
        scratch_shapes=scratch,
        compiler_params=pltpu.CompilerParams(vmem_limit_bytes=limit * 1024 * 1024),
        cost_estimate=estimate,
        name=name,
    )(*operands)


def inverse_rms(u_ref, eps=1e-05):
    rows, width = u_ref.shape
    total = jnp.zeros((rows, LANES), F32)
    for c in range(width // LANES):
        part = u_ref[:, c * LANES : (c + 1) * LANES].astype(F32)
        total = total + part * part
    return lax.rsqrt(jnp.sum(total, axis=1, keepdims=True) / width + eps)


def norm_kernel(u_hbm, gain_hbm, out_hbm, u_ref, gain_ref, out_ref, sems):
    blocks, groups, rows, chans = out_ref.shape
    span = [pl.ds(b * rows, rows) for b in range(blocks)]
    gain_copy, *u_copies = load(
        [(gain_hbm, gain_ref)] + [(u_hbm.at[span[b]], u_ref.at[b]) for b in range(blocks)], sems
    )
    gain_copy.wait()
    out_copies = []
    for b in range(blocks):
        u_copies[b].wait()
        inv = inverse_rms(u_ref.at[b])
        for c in range(groups):
            cols = slice(c * chans, (c + 1) * chans)
            normal = u_ref[b, :, cols].astype(F32) * inv
            out_ref[b, c] = (normal * gain_ref[:, cols]).astype(BF16)
        copy = pltpu.make_async_copy(out_ref.at[b], out_hbm.at[:, span[b]], sems.at[1 + blocks + b])
        copy.start()
        out_copies.append(copy)
    for copy in out_copies:
        copy.wait()


def norm_rows(u_rows, gain, groups):
    rows, width = u_rows.shape
    chans, blocks = width // groups, rows // ROW_BLOCK
    return call(
        norm_kernel,
        [jax.ShapeDtypeStruct((groups, rows, chans), BF16)],
        [
            pltpu.VMEM((blocks, ROW_BLOCK, width), BF16),
            pltpu.VMEM((1, width), F32),
            pltpu.VMEM((blocks, groups, ROW_BLOCK, chans), BF16),
            pltpu.SemaphoreType.DMA((1 + 2 * blocks,)),
        ],
        "norm_rows",
        cost(8 * rows * width, 4 * rows * width),
        [pl.ANY] * 2,
        [pl.ANY],
        (u_rows, gain),
        60,
    )[0]


def final_kernel(u_ref, gain_ref, grad_ref, out_hbm, out_ref, sems):
    blocks, rows, _ = out_ref.shape
    groups, _, chans = grad_ref.shape
    width = groups * chans
    out_copies = []
    for b in range(blocks):
        span = pl.ds(b * rows, rows)
        inv = inverse_rms(u_ref.at[span])
        total = jnp.zeros((rows, chans), F32)
        for c in range(groups):
            cols = slice(c * chans, (c + 1) * chans)
            normal = u_ref[span, cols].astype(F32) * inv
            total = total + normal * (gain_ref[:, cols] * grad_ref[c, span, :].astype(F32))
        project = jnp.sum(total, axis=1, keepdims=True) / width
        for c in range(groups):
            cols = slice(c * chans, (c + 1) * chans)
            normal = u_ref[span, cols].astype(F32) * inv
            scaled = gain_ref[:, cols] * grad_ref[c, span, :].astype(F32)
            out_ref[b, :, cols] = (inv * (scaled - normal * project)).astype(BF16)
        copy = pltpu.make_async_copy(out_ref.at[b], out_hbm.at[span], sems.at[b])
        copy.start()
        out_copies.append(copy)
    for copy in out_copies:
        copy.wait()


def final_rows(u_rows, gain, grad_rows):
    rows, width = u_rows.shape
    blocks = rows // ROW_BLOCK
    return call(
        final_kernel,
        [jax.ShapeDtypeStruct((rows, width), BF16)],
        [
            pltpu.VMEM((blocks, ROW_BLOCK, width), BF16),
            pltpu.SemaphoreType.DMA((blocks,)),
        ],
        "final_rows",
        cost(16 * rows * width, 6 * rows * width),
        [pltpu.VMEM] * 3,
        [pl.ANY],
        (u_rows, gain, grad_rows),
    )[0]


def doc_starts(lens_ref):
    starts, at = [], jnp.int32(0)
    for k in range(lens_ref.shape[0] - 1):
        at = at + lens_ref[k]
        starts.append(at)
    return starts


def sort_down(codes):
    codes = list(codes)
    for end in range(len(codes) - 1, 0, -1):
        for k in range(end):
            high = jnp.maximum(codes[k], codes[k + 1])
            low = jnp.minimum(codes[k], codes[k + 1])
            codes[k], codes[k + 1] = high, low
    return codes


def cut_codes(starts, streams, base, seg_len):
    codes = []
    for start, stream in zip(starts, streams):
        place = start - base
        inside = (place >= 0) & (place < SEGS * seg_len)
        code = (place % seg_len) * 16 + place // seg_len
        codes.append(jnp.where(inside, code, 15) * 2 + stream)
    return sort_down(codes)


def any_start(starts, first, count):
    found = jnp.bool_(False)
    for start in starts:
        found = found | ((start >= first) & (start < first + count))
    return found


def time_loop(cuts_ref, seg_len, step, cut, carry):
    def piece(p, state):
        top, inner = state
        code = cuts_ref[p]
        low = code // 32
        count = top - low
        full = count // UNROLL

        def many(k, value):
            first = top - (k + 1) * UNROLL
            for j in range(UNROLL - 1, -1, -1):
                value = step(first + j, value)
            return value

        def one(k, value):
            return step(top - full * UNROLL - 1 - k, value)

        inner = lax.fori_loop(0, full, many, inner)
        inner = lax.fori_loop(0, count - full * UNROLL, one, inner)
        inner = cut((code // 2) % 16, code % 2, inner)
        return (low, inner)

    return lax.fori_loop(0, cuts_ref.shape[0], piece, (jnp.int32(seg_len), carry))[1]


def order_matrix(steps, to_steps):
    size = SEGS * steps
    row = lax.broadcasted_iota(jnp.int32, (size, size), 0)
    col = lax.broadcasted_iota(jnp.int32, (size, size), 1)
    by_step, by_segment = (row, col) if to_steps else (col, row)
    return (by_segment == by_step % SEGS * steps + by_step // SEGS).astype(F32).astype(BF16)


def block_steps(tokens):
    return min(STEPS, tokens // SEGS)


def to_steps(source_ref, target_ref, order_ref):
    halves, tokens, _ = target_ref.shape
    steps, seg_len = block_steps(tokens), tokens // SEGS

    def body(b, _):
        rows = [
            source_ref[pl.ds(pl.multiple_of(s * seg_len + b * steps, steps), steps), :] for s in range(SEGS)
        ]
        block = jnp.dot(order_ref[...], jnp.concatenate(rows, axis=0), preferred_element_type=F32)
        size = SEGS * steps
        for h in range(halves):
            target_ref[h, pl.ds(pl.multiple_of(b * size, size), size), :] = block[
                :, h * LANES : (h + 1) * LANES
            ]
        return 0

    lax.fori_loop(0, seg_len // steps, body, 0)


def from_steps(source_ref, target_ref, order_ref):
    halves, tokens, _ = source_ref.shape
    steps, seg_len = block_steps(tokens), tokens // SEGS

    def body(b, _):
        size = SEGS * steps
        rows = pl.ds(pl.multiple_of(b * size, size), size)
        block = jnp.concatenate([source_ref[h, rows, :].astype(BF16) for h in range(halves)], axis=1)
        block = jnp.dot(order_ref[...], block, preferred_element_type=F32).astype(BF16)
        for s in range(SEGS):
            target_ref[pl.ds(pl.multiple_of(s * seg_len + b * steps, steps), steps), :] = block[
                s * steps : (s + 1) * steps
            ]
        return 0

    lax.fori_loop(0, seg_len // steps, body, 0)


def step_rows(i):
    return pl.ds(pl.multiple_of(i * SEGS, SEGS), SEGS)


def spread(ref, r, cols):
    return jnp.broadcast_to(ref[r : r + 1, cols], (SEGS, LANES))


def segment(ref, s, modes):
    rows = slice(s * modes, (s + 1) * modes)
    return jnp.concatenate([ref[h, rows, :] for h in range(ref.shape[0])], axis=1)


def put_segment(ref, s, modes, value):
    for h in range(ref.shape[0]):
        ref[h, s * modes : (s + 1) * modes, :] = value[:, h * LANES : (h + 1) * LANES]


def store_cuts(cuts_ref, codes):
    for k, code in enumerate(codes):
        cuts_ref[k] = code
    cuts_ref[len(codes)] = jnp.int32(30)


def leave_kernel(
    lens_ref, rates_ref, residues_ref, skip_ref, grad_ref, seg_ref, dev_ref, coef_ref,
    wide_ref, order_ref, cuts_ref,
):
    tokens, chans = grad_ref.shape
    modes = rates_ref.shape[0]
    seg_len = tokens // SEGS
    base = lax.axis_index("ctx") * tokens
    starts = doc_starts(lens_ref)
    store_cuts(cuts_ref, cut_codes(starts, [0] * len(starts), base, seg_len))
    order_ref[...] = order_matrix(block_steps(tokens), True)
    to_steps(grad_ref, wide_ref, order_ref)
    rates = rates_ref[...]
    decay_all = jnp.exp(-rates)
    mode_scale = jnp.sqrt(1.0 - decay_all * decay_all)
    coef_ref[:modes] = decay_all
    coef_ref[modes : 2 * modes] = mode_scale
    coef_ref[2 * modes : 3 * modes] = residues_ref[...] * mode_scale
    coef_ref[3 * modes :] = jnp.broadcast_to(skip_ref[...], (SEGS, chans))
    row = lax.broadcasted_iota(jnp.int32, (SEGS, LANES), 0)
    for h in range(chans // LANES):
        cols = slice(h * LANES, (h + 1) * LANES)
        decay = [spread(coef_ref, r, cols) for r in range(modes)]

        def step(i, state):
            grad = wide_ref[h, step_rows(i), :]
            return tuple(grad + decay[r] * state[r] for r in range(modes))

        def cut(place, stream, state):
            hold = row != place
            return tuple(jnp.where(hold, part, 0.0) for part in state)

        zero = jnp.zeros((SEGS, LANES), F32)
        state = time_loop(cuts_ref, seg_len, step, cut, (zero,) * modes)
        for r in range(modes):
            seg_ref[h, pl.ds(r, SEGS, stride=modes), :] = decay[r] * state[r]
    through = jnp.exp(-rates * float(seg_len))
    leaving = segment(seg_ref, SEGS - 1, modes)
    for s in range(SEGS - 2, -1, -1):
        kept = jnp.where(any_start(starts, base + s * seg_len, seg_len), 0.0, 1.0)
        leaving = segment(seg_ref, s, modes) + (through * kept) * leaving
    dev_ref[...] = leaving


def state_scratch(docs, modes, tokens, chans):
    halves, size = chans // LANES, SEGS * block_steps(tokens)
    return {
        "cuts": pltpu.SMEM((docs,), jnp.int32),
        "narrow": pltpu.VMEM((tokens, chans), BF16),
        "wide": pltpu.VMEM((halves, tokens, LANES), F32),
        "order": pltpu.VMEM((size, size), BF16),
        "segs": pltpu.VMEM((halves, SEGS * modes, LANES), F32),
        "weights": pltpu.VMEM((modes, SEGS, LANES), F32),
        "total": pltpu.VMEM((2, modes, SEGS, chans), F32),
        "sems": pltpu.SemaphoreType.DMA((1,)),
    }


def leave(doc_lengths, rates, residues, skip, grad_out):
    modes, chans = rates.shape
    tokens = grad_out.shape[0]
    kinds = state_scratch(doc_lengths.shape[0], modes, tokens, chans)
    return call(
        leave_kernel,
        [
            jax.ShapeDtypeStruct((chans // LANES, SEGS * modes, LANES), F32),
            jax.ShapeDtypeStruct((modes, chans), F32),
            jax.ShapeDtypeStruct((3 * modes + SEGS, chans), F32),
        ],
        [kinds[k] for k in ("wide", "order", "cuts")],
        "leave",
        cost(2 * tokens * chans * modes, 2 * tokens * chans),
        [pltpu.SMEM] + [pltpu.VMEM] * 4,
        [pltpu.VMEM] * 3,
        (doc_lengths, rates, residues, skip, grad_out),
    )


def back_kernel(window, lens_ref, streams_ref, rates_ref, coef_ref, grad_ref, x_ref, seg_ref, *refs):
    later = refs[:-12]
    (out_hbm, residue_ref, out_ref, arrive_ref, wide_ref, x_wide_ref, conv_ref, weight_ref, total_ref,
     order_ref, cuts_ref, sems) = refs[-12:]
    tokens, chans = grad_ref.shape
    modes = rates_ref.shape[0]
    seg_len = tokens // SEGS
    here, last = lax.axis_index("ctx"), lax.axis_size("ctx")
    base = here * tokens
    starts = doc_starts(lens_ref)
    streams = [streams_ref[k] for k in range(len(starts) + 1)]
    store_cuts(cuts_ref, cut_codes(starts, streams[1:], base, seg_len))
    rates = rates_ref[...]
    through = jnp.exp(-rates * float(tokens))
    arriving = jnp.zeros((modes, chans), F32)
    for k in range(len(later), 0, -1):
        kept = jnp.where(any_start(starts, (here + k) * tokens, tokens), 0.0, 1.0)
        arriving = later[k - 1][...] + (through * kept) * arriving
        arriving = jnp.where(here + k < last, arriving, 0.0)
    through = jnp.exp(-rates * float(seg_len))
    put_segment(arrive_ref, SEGS - 1, modes, arriving)
    for s in range(SEGS - 1, 0, -1):
        kept = jnp.where(any_start(starts, base + s * seg_len, seg_len), 0.0, 1.0)
        arriving = segment(seg_ref, s, modes) + (through * kept) * arriving
        put_segment(arrive_ref, s - 1, modes, arriving)
    order_ref[...] = order_matrix(block_steps(tokens), True)
    to_steps(grad_ref, wide_ref, order_ref)
    to_steps(x_ref, x_wide_ref, order_ref)
    total_ref[...] = jnp.zeros_like(total_ref)
    row = lax.broadcasted_iota(jnp.int32, (SEGS, LANES), 0)
    first = base + row * seg_len
    stream_at = jnp.full((SEGS, LANES), streams[0], jnp.int32)
    for start, stream in zip(starts, streams[1:]):
        stream_at = jnp.where(first >= start, stream, stream_at)
    for h in range(chans // LANES):
        cols = slice(h * LANES, (h + 1) * LANES)
        decay = [spread(coef_ref, r, cols) for r in range(modes)]
        for r in range(modes):
            weight_ref[r] = spread(coef_ref, 2 * modes + r, cols)
        skip = coef_ref[3 * modes :, cols]

        def step(i, carry):
            state, total = carry
            rows = step_rows(i)
            grad = wide_ref[h, rows, :]
            x = x_wide_ref[h, rows, :]
            sums = [skip * grad, None, None, None]
            new_state, new_total = [], []
            for r in range(modes):
                back = grad + state[r]
                term = weight_ref[r] * back
                sums[r % 4] = term if sums[r % 4] is None else sums[r % 4] + term
                new_total.append(total[r] + x * back)
                new_state.append(decay[r] * back)
            conv_ref[h, rows, :] = (sums[0] + sums[1]) + (sums[2] + sums[3])
            return (tuple(new_state), tuple(new_total))

        def cut(place, stream, carry):
            state, total = carry
            hold = row != place
            for r in range(modes):
                total_ref[stream, r, :, cols] += jnp.where(hold, 0.0, total[r])
            return (
                tuple(jnp.where(hold, part, 0.0) for part in state),
                tuple(jnp.where(hold, part, 0.0) for part in total),
            )

        zero = jnp.zeros((SEGS, LANES), F32)
        entry = tuple(arrive_ref[h, pl.ds(r, SEGS, stride=modes), :] for r in range(modes))
        _, total = time_loop(cuts_ref, seg_len, step, cut, (entry, (zero,) * modes))
        for s in range(2):
            for r in range(modes):
                total_ref[s, r, :, cols] += jnp.where(stream_at == s, total[r], 0.0)
    order_ref[...] = order_matrix(block_steps(tokens), False)
    from_steps(conv_ref, out_ref, order_ref)
    copy = pltpu.make_async_copy(out_ref, out_hbm, sems.at[0])
    copy.start()
    scale = coef_ref[modes : 2 * modes] / math.sqrt(window)
    for s in range(2):
        residue_ref[s] = (jnp.sum(total_ref[s], axis=1) * scale).astype(BF16)
    copy.wait()


def back_pass(doc_lengths, doc_streams, rates, coef, grad_out, x_cols, seg_leaving, later, window):
    modes, chans = rates.shape
    tokens = grad_out.shape[0]
    kinds = state_scratch(doc_lengths.shape[0], modes, tokens, chans)
    names = ("narrow", "segs", "wide", "wide", "wide", "weights", "total", "order", "cuts", "sems")

    def kernel(*refs):
        back_kernel(window, *refs)

    return call(
        kernel,
        [
            jax.ShapeDtypeStruct((tokens, chans), BF16),
            jax.ShapeDtypeStruct((2, modes, chans), BF16),
        ],
        [kinds[k] for k in names],
        "back_pass",
        cost(6 * tokens * chans * modes, 6 * tokens * chans),
        [pltpu.SMEM] * 2 + [pltpu.VMEM] * (5 + len(later)),
        [pl.ANY, pltpu.VMEM],
        (doc_lengths, doc_streams, rates, coef, grad_out, x_cols, seg_leaving, *later),
        24,
    )


def from_later(value, axis):
    count = lax.axis_size(axis)
    return [
        lax.ppermute(value, axis, [((i + k) % count, i) for i in range(count)])
        for k in range(1, count // 2 + 1)
    ]


def sum_over(value, axis):
    count = lax.axis_size(axis)
    half = count // 2
    parts = [value] + [
        lax.ppermute(value, axis, [(i, i // half * half + (i + k) % half) for i in range(count)])
        for k in range(1, half)
    ]
    parts = [part.astype(F32) for part in parts]
    while len(parts) > 1:
        middle = len(parts) // 2
        parts = [a + b for a, b in zip(parts[:middle], parts[middle:])]
    other = lax.ppermute(parts[0], axis, [(i, (i + half) % count) for i in range(count)])
    return parts[0] + other


def local(u_rows, gain, skip, residues, rates, grad_out, doc_lengths, doc_streams):
    ctx, groups = lax.axis_size("ctx"), lax.axis_size("ch")
    tokens, chans = grad_out.shape
    gain = gain[None, :]
    rates, residues = rates.T, residues.T
    x_send = norm_rows(u_rows, gain, groups)
    x_send, rates = lax.optimization_barrier((x_send, rates))
    x_cols = lax.all_to_all(x_send, "ch", split_axis=0, concat_axis=0, tiled=True)
    x_cols = x_cols.reshape(tokens, chans)
    seg_leaving, dev_leaving, coef = leave(doc_lengths, rates, residues, skip[None, :], grad_out)
    later = from_later(dev_leaving, "ctx")
    normed_grad, parts = back_pass(
        doc_lengths, doc_streams, rates, coef, grad_out, x_cols, seg_leaving, later, tokens * ctx
    )
    grad_rows = lax.all_to_all(
        normed_grad.reshape(groups, tokens // groups, chans), "ch", split_axis=0, concat_axis=0, tiled=True
    )
    residue_grad = sum_over(parts, "ctx").transpose(0, 2, 1)
    input_grad = final_rows(u_rows, gain, grad_rows)
    return (input_grad, residue_grad)


def solution(mesh):
    return jax.shard_map(
        local,
        mesh=mesh,
        in_specs=(
            P(("ctx", "ch"), None),
            P(),
            P("ch"),
            P("ch", None),
            P("ch", None),
            P("ctx", "ch"),
            P(),
            P(),
        ),
        out_specs=(P(("ctx", "ch"), None), P(None, "ch", None)),
        check_vma=False,
    )
```

```python
import math

import jax
import jax.numpy as jnp
from jax import lax
from jax.experimental import pallas as pl
from jax.experimental.pallas import tpu as pltpu
from jax.sharding import PartitionSpec as P

F32 = jnp.float32
BF16 = jnp.bfloat16
SEGS = 8
LANES = 128
UNROLL = 16
STEPS = 32
ROW_BLOCK = 16


def cost(flops, size):
    return pl.CostEstimate(flops=flops, bytes_accessed=size, transcendentals=0)


def load(pairs, sems):
    copies = [pltpu.make_async_copy(a, b, sems.at[k]) for k, (a, b) in enumerate(pairs)]
    for copy in copies:
        copy.start()
    return copies


def call(kernel, outs, scratch, name, estimate, spaces, out_spaces, operands, limit=16):
    return pl.pallas_call(
        kernel,
        in_specs=[pl.BlockSpec(memory_space=space) for space in spaces],
        out_specs=[pl.BlockSpec(memory_space=space) for space in out_spaces],
        out_shape=outs,
        scratch_shapes=scratch,
        compiler_params=pltpu.CompilerParams(vmem_limit_bytes=limit * 1024 * 1024),
        cost_estimate=estimate,
        name=name,
    )(*operands)


def inverse_rms(u_ref, eps=1e-05):
    rows, width = u_ref.shape
    total = jnp.zeros((rows, LANES), F32)
    for c in range(width // LANES):
        part = u_ref[:, c * LANES : (c + 1) * LANES].astype(F32)
        total = total + part * part
    return lax.rsqrt(jnp.sum(total, axis=1, keepdims=True) / width + eps)


def norm_kernel(u_hbm, gain_hbm, out_hbm, u_ref, gain_ref, out_ref, sems):
    blocks, groups, rows, chans = out_ref.shape
    span = [pl.ds(b * rows, rows) for b in range(blocks)]
    gain_copy, *u_copies = load(
        [(gain_hbm, gain_ref)] + [(u_hbm.at[span[b]], u_ref.at[b]) for b in range(blocks)], sems
    )
    gain_copy.wait()
    out_copies = []
    for b in range(blocks):
        u_copies[b].wait()
        inv = inverse_rms(u_ref.at[b])
        for c in range(groups):
            cols = slice(c * chans, (c + 1) * chans)
            normal = u_ref[b, :, cols].astype(F32) * inv
            out_ref[b, c] = (normal * gain_ref[:, cols]).astype(BF16)
        copy = pltpu.make_async_copy(out_ref.at[b], out_hbm.at[:, span[b]], sems.at[1 + blocks + b])
        copy.start()
        out_copies.append(copy)
    for copy in out_copies:
        copy.wait()


def norm_rows(u_rows, gain, groups):
    rows, width = u_rows.shape
    chans, blocks = width // groups, rows // ROW_BLOCK
    return call(
        norm_kernel,
        [jax.ShapeDtypeStruct((groups, rows, chans), BF16)],
        [
            pltpu.VMEM((blocks, ROW_BLOCK, width), BF16),
            pltpu.VMEM((1, width), F32),
            pltpu.VMEM((blocks, groups, ROW_BLOCK, chans), BF16),
            pltpu.SemaphoreType.DMA((1 + 2 * blocks,)),
        ],
        "norm_rows",
        cost(8 * rows * width, 4 * rows * width),
        [pl.ANY] * 2,
        [pl.ANY],
        (u_rows, gain),
        60,
    )[0]


def final_kernel(u_ref, gain_ref, grad_ref, out_hbm, out_ref, sems):
    blocks, rows, _ = out_ref.shape
    groups, _, chans = grad_ref.shape
    width = groups * chans
    out_copies = []
    for b in range(blocks):
        span = pl.ds(b * rows, rows)
        inv = inverse_rms(u_ref.at[span])
        total = jnp.zeros((rows, chans), F32)
        for c in range(groups):
            cols = slice(c * chans, (c + 1) * chans)
            normal = u_ref[span, cols].astype(F32) * inv
            total = total + normal * (gain_ref[:, cols] * grad_ref[c, span, :].astype(F32))
        project = jnp.sum(total, axis=1, keepdims=True) / width
        for c in range(groups):
            cols = slice(c * chans, (c + 1) * chans)
            normal = u_ref[span, cols].astype(F32) * inv
            scaled = gain_ref[:, cols] * grad_ref[c, span, :].astype(F32)
            out_ref[b, :, cols] = (inv * (scaled - normal * project)).astype(BF16)
        copy = pltpu.make_async_copy(out_ref.at[b], out_hbm.at[span], sems.at[b])
        copy.start()
        out_copies.append(copy)
    for copy in out_copies:
        copy.wait()


def final_rows(u_rows, gain, grad_rows):
    rows, width = u_rows.shape
    blocks = rows // ROW_BLOCK
    return call(
        final_kernel,
        [jax.ShapeDtypeStruct((rows, width), BF16)],
        [
            pltpu.VMEM((blocks, ROW_BLOCK, width), BF16),
            pltpu.SemaphoreType.DMA((blocks,)),
        ],
        "final_rows",
        cost(16 * rows * width, 6 * rows * width),
        [pltpu.VMEM] * 3,
        [pl.ANY],
        (u_rows, gain, grad_rows),
    )[0]


def doc_starts(lens_ref):
    starts, at = [], jnp.int32(0)
    for k in range(lens_ref.shape[0] - 1):
        at = at + lens_ref[k]
        starts.append(at)
    return starts


def sort_down(codes):
    codes = list(codes)
    for end in range(len(codes) - 1, 0, -1):
        for k in range(end):
            high = jnp.maximum(codes[k], codes[k + 1])
            low = jnp.minimum(codes[k], codes[k + 1])
            codes[k], codes[k + 1] = high, low
    return codes


def cut_codes(starts, streams, base, seg_len):
    codes = []
    for start, stream in zip(starts, streams):
        place = start - base
        inside = (place >= 0) & (place < SEGS * seg_len)
        code = (place % seg_len) * 16 + place // seg_len
        codes.append(jnp.where(inside, code, 15) * 2 + stream)
    return sort_down(codes)


def any_start(starts, first, count):
    found = jnp.bool_(False)
    for start in starts:
        found = found | ((start >= first) & (start < first + count))
    return found


def time_loop(cuts_ref, seg_len, step, cut, carry):
    def piece(p, state):
        top, inner = state
        code = cuts_ref[p]
        low = code // 32
        count = top - low
        full = count // UNROLL

        def many(k, value):
            first = top - (k + 1) * UNROLL
            for j in range(UNROLL - 1, -1, -1):
                value = step(first + j, value)
            return value

        def one(k, value):
            return step(top - full * UNROLL - 1 - k, value)

        inner = lax.fori_loop(0, full, many, inner)
        inner = lax.fori_loop(0, count - full * UNROLL, one, inner)
        inner = cut((code // 2) % 16, code % 2, inner)
        return (low, inner)

    return lax.fori_loop(0, cuts_ref.shape[0], piece, (jnp.int32(seg_len), carry))[1]


def order_matrix(steps, to_steps):
    size = SEGS * steps
    row = lax.broadcasted_iota(jnp.int32, (size, size), 0)
    col = lax.broadcasted_iota(jnp.int32, (size, size), 1)
    by_step, by_segment = (row, col) if to_steps else (col, row)
    return (by_segment == by_step % SEGS * steps + by_step // SEGS).astype(F32).astype(BF16)


def block_steps(tokens):
    return min(STEPS, tokens // SEGS)


def to_steps(source_ref, target_ref, order_ref):
    halves, tokens, _ = target_ref.shape
    steps, seg_len = block_steps(tokens), tokens // SEGS

    def body(b, _):
        rows = [
            source_ref[pl.ds(pl.multiple_of(s * seg_len + b * steps, steps), steps), :] for s in range(SEGS)
        ]
        block = jnp.dot(order_ref[...], jnp.concatenate(rows, axis=0), preferred_element_type=F32)
        size = SEGS * steps
        for h in range(halves):
            target_ref[h, pl.ds(pl.multiple_of(b * size, size), size), :] = block[
                :, h * LANES : (h + 1) * LANES
            ]
        return 0

    lax.fori_loop(0, seg_len // steps, body, 0)


def from_steps(source_ref, target_ref, order_ref):
    halves, tokens, _ = source_ref.shape
    steps, seg_len = block_steps(tokens), tokens // SEGS

    def body(b, _):
        size = SEGS * steps
        rows = pl.ds(pl.multiple_of(b * size, size), size)
        block = jnp.concatenate([source_ref[h, rows, :].astype(BF16) for h in range(halves)], axis=1)
        block = jnp.dot(order_ref[...], block, preferred_element_type=F32).astype(BF16)
        for s in range(SEGS):
            target_ref[pl.ds(pl.multiple_of(s * seg_len + b * steps, steps), steps), :] = block[
                s * steps : (s + 1) * steps
            ]
        return 0

    lax.fori_loop(0, seg_len // steps, body, 0)


def step_rows(i):
    return pl.ds(pl.multiple_of(i * SEGS, SEGS), SEGS)


def spread(ref, r, cols):
    return jnp.broadcast_to(ref[r : r + 1, cols], (SEGS, LANES))


def segment(ref, s, modes):
    rows = slice(s * modes, (s + 1) * modes)
    return jnp.concatenate([ref[h, rows, :] for h in range(ref.shape[0])], axis=1)


def put_segment(ref, s, modes, value):
    for h in range(ref.shape[0]):
        ref[h, s * modes : (s + 1) * modes, :] = value[:, h * LANES : (h + 1) * LANES]


def store_cuts(cuts_ref, codes):
    for k, code in enumerate(codes):
        cuts_ref[k] = code
    cuts_ref[len(codes)] = jnp.int32(30)


def leave_kernel(
    lens_ref, streams_ref, rates_ref, residues_ref, skip_ref, grad_ref, seg_ref, dev_ref, coef_ref,
    wide_ref, order_ref, cuts_ref,
):
    tokens, chans = grad_ref.shape
    modes = rates_ref.shape[0]
    seg_len = tokens // SEGS
    base = lax.axis_index("ctx") * tokens
    starts = doc_starts(lens_ref)
    streams = [streams_ref[k] for k in range(len(starts) + 1)]
    store_cuts(cuts_ref, cut_codes(starts, streams[1:], base, seg_len))
    order_ref[...] = order_matrix(block_steps(tokens), True)
    to_steps(grad_ref, wide_ref, order_ref)
    rates = rates_ref[...]
    decay_all = jnp.exp(-rates)
    mode_scale = jnp.sqrt(1.0 - decay_all * decay_all)
    coef_ref[:modes] = decay_all
    coef_ref[modes : 2 * modes] = mode_scale
    coef_ref[2 * modes : 3 * modes] = residues_ref[...] * mode_scale
    coef_ref[3 * modes :] = jnp.broadcast_to(skip_ref[...], (SEGS, chans))
    row = lax.broadcasted_iota(jnp.int32, (SEGS, LANES), 0)
    for h in range(chans // LANES):
        cols = slice(h * LANES, (h + 1) * LANES)
        decay = [spread(coef_ref, r, cols) for r in range(modes)]

        def step(i, state):
            grad = wide_ref[h, step_rows(i), :]
            return tuple(grad + decay[r] * state[r] for r in range(modes))

        def cut(place, stream, state):
            hold = row != place
            return tuple(jnp.where(hold, part, 0.0) for part in state)

        zero = jnp.zeros((SEGS, LANES), F32)
        state = time_loop(cuts_ref, seg_len, step, cut, (zero,) * modes)
        for r in range(modes):
            seg_ref[h, pl.ds(r, SEGS, stride=modes), :] = decay[r] * state[r]
    through = jnp.exp(-rates * float(seg_len))
    leaving = segment(seg_ref, SEGS - 1, modes)
    for s in range(SEGS - 2, -1, -1):
        kept = jnp.where(any_start(starts, base + s * seg_len, seg_len), 0.0, 1.0)
        leaving = segment(seg_ref, s, modes) + (through * kept) * leaving
    dev_ref[...] = leaving


def state_scratch(docs, modes, tokens, chans):
    halves, size = chans // LANES, SEGS * block_steps(tokens)
    return {
        "cuts": pltpu.SMEM((docs,), jnp.int32),
        "narrow": pltpu.VMEM((tokens, chans), BF16),
        "wide": pltpu.VMEM((halves, tokens, LANES), F32),
        "order": pltpu.VMEM((size, size), BF16),
        "total": pltpu.VMEM((2, modes, SEGS, chans), F32),
        "sems": pltpu.SemaphoreType.DMA((1,)),
    }


def leave(doc_lengths, doc_streams, rates, residues, skip, grad_out):
    modes, chans = rates.shape
    tokens = grad_out.shape[0]
    kinds = state_scratch(doc_lengths.shape[0], modes, tokens, chans)
    return call(
        leave_kernel,
        [
            jax.ShapeDtypeStruct((chans // LANES, SEGS * modes, LANES), F32),
            jax.ShapeDtypeStruct((modes, chans), F32),
            jax.ShapeDtypeStruct((3 * modes + SEGS, chans), F32),
        ],
        [kinds[k] for k in ("wide", "order", "cuts")],
        "leave",
        cost(2 * tokens * chans * modes, 2 * tokens * chans),
        [pltpu.SMEM] * 2 + [pltpu.VMEM] * 4,
        [pltpu.VMEM] * 3,
        (doc_lengths, doc_streams, rates, residues, skip, grad_out),
    )


def back_kernel(lens_ref, streams_ref, rates_ref, coef_ref, grad_ref, seg_ref, *refs):
    later = refs[:-8]
    out_hbm, arrive_ref, out_ref, wide_ref, conv_ref, order_ref, cuts_ref, sems = refs[-8:]
    tokens, chans = grad_ref.shape
    modes = rates_ref.shape[0]
    seg_len = tokens // SEGS
    here, last = lax.axis_index("ctx"), lax.axis_size("ctx")
    base = here * tokens
    starts = doc_starts(lens_ref)
    streams = [streams_ref[k] for k in range(len(starts) + 1)]
    store_cuts(cuts_ref, cut_codes(starts, streams[1:], base, seg_len))
    rates = rates_ref[...]
    through = jnp.exp(-rates * float(tokens))
    arriving = jnp.zeros((modes, chans), F32)
    for k in range(len(later), 0, -1):
        kept = jnp.where(any_start(starts, (here + k) * tokens, tokens), 0.0, 1.0)
        arriving = later[k - 1][...] + (through * kept) * arriving
        arriving = jnp.where(here + k < last, arriving, 0.0)
    through = jnp.exp(-rates * float(seg_len))
    put_segment(arrive_ref, SEGS - 1, modes, arriving)
    for s in range(SEGS - 1, 0, -1):
        kept = jnp.where(any_start(starts, base + s * seg_len, seg_len), 0.0, 1.0)
        arriving = segment(seg_ref, s, modes) + (through * kept) * arriving
        put_segment(arrive_ref, s - 1, modes, arriving)
    order_ref[...] = order_matrix(block_steps(tokens), True)
    to_steps(grad_ref, wide_ref, order_ref)
    row = lax.broadcasted_iota(jnp.int32, (SEGS, LANES), 0)
    for h in range(chans // LANES):
        cols = slice(h * LANES, (h + 1) * LANES)
        decay = [spread(coef_ref, r, cols) for r in range(modes)]
        weight = [spread(coef_ref, 2 * modes + r, cols) for r in range(modes)]
        skip = coef_ref[3 * modes :, cols]

        def step(i, state):
            rows = step_rows(i)
            grad = wide_ref[h, rows, :]
            sums = [skip * grad, None, None, None]
            new_state = []
            for r in range(modes):
                back = grad + state[r]
                term = weight[r] * back
                sums[r % 4] = term if sums[r % 4] is None else sums[r % 4] + term
                new_state.append(decay[r] * back)
            conv_ref[h, rows, :] = (sums[0] + sums[1]) + (sums[2] + sums[3])
            return tuple(new_state)

        def cut(place, stream, state):
            hold = row != place
            return tuple(jnp.where(hold, part, 0.0) for part in state)

        entry = tuple(arrive_ref[h, pl.ds(r, SEGS, stride=modes), :] for r in range(modes))
        time_loop(cuts_ref, seg_len, step, cut, entry)
    order_ref[...] = order_matrix(block_steps(tokens), False)
    from_steps(conv_ref, out_ref, order_ref)
    copy = pltpu.make_async_copy(out_ref, out_hbm, sems.at[0])
    copy.start()
    copy.wait()


def back_pass(doc_lengths, doc_streams, rates, coef, grad_out, seg_leaving, later):
    modes, chans = rates.shape
    tokens = grad_out.shape[0]
    kinds = state_scratch(doc_lengths.shape[0], modes, tokens, chans)
    return call(
        back_kernel,
        [
            jax.ShapeDtypeStruct((tokens, chans), BF16),
            jax.ShapeDtypeStruct((chans // LANES, SEGS * modes, LANES), F32),
        ],
        [kinds[k] for k in ("narrow", "wide", "wide", "order", "cuts", "sems")],
        "back_pass",
        cost(4 * tokens * chans * modes, 4 * tokens * chans),
        [pltpu.SMEM] * 2 + [pltpu.VMEM] * (4 + len(later)),
        [pl.ANY, pltpu.VMEM],
        (doc_lengths, doc_streams, rates, coef, grad_out, seg_leaving, *later),
    )


def residue_kernel(
    window, lens_ref, streams_ref, coef_ref, grad_ref, x_ref, arrive_ref, residue_ref,
    wide_ref, x_wide_ref, total_ref, order_ref, cuts_ref,
):
    tokens, chans = grad_ref.shape
    modes = residue_ref.shape[1]
    seg_len = tokens // SEGS
    base = lax.axis_index("ctx") * tokens
    starts = doc_starts(lens_ref)
    streams = [streams_ref[k] for k in range(len(starts) + 1)]
    store_cuts(cuts_ref, cut_codes(starts, streams[1:], base, seg_len))
    order_ref[...] = order_matrix(block_steps(tokens), True)
    to_steps(grad_ref, wide_ref, order_ref)
    to_steps(x_ref, x_wide_ref, order_ref)
    total_ref[...] = jnp.zeros_like(total_ref)
    row = lax.broadcasted_iota(jnp.int32, (SEGS, LANES), 0)
    first = base + row * seg_len
    stream_at = jnp.full((SEGS, LANES), streams[0], jnp.int32)
    for start, stream in zip(starts, streams[1:]):
        stream_at = jnp.where(first >= start, stream, stream_at)
    for h in range(chans // LANES):
        cols = slice(h * LANES, (h + 1) * LANES)
        decay = [spread(coef_ref, r, cols) for r in range(modes)]

        def step(i, carry):
            state, total = carry
            rows = step_rows(i)
            grad = wide_ref[h, rows, :]
            x = x_wide_ref[h, rows, :]
            back = [grad + part for part in state]
            total = tuple(total[r] + x * back[r] for r in range(modes))
            return (tuple(decay[r] * back[r] for r in range(modes)), total)

        def cut(place, stream, carry):
            state, total = carry
            hold = row != place
            for r in range(modes):
                total_ref[stream, r, :, cols] += jnp.where(hold, 0.0, total[r])
            return (
                tuple(jnp.where(hold, part, 0.0) for part in state),
                tuple(jnp.where(hold, part, 0.0) for part in total),
            )

        zero = jnp.zeros((SEGS, LANES), F32)
        entry = tuple(arrive_ref[h, pl.ds(r, SEGS, stride=modes), :] for r in range(modes))
        _, total = time_loop(cuts_ref, seg_len, step, cut, (entry, (zero,) * modes))
        for s in range(2):
            for r in range(modes):
                total_ref[s, r, :, cols] += jnp.where(stream_at == s, total[r], 0.0)
    scale = coef_ref[modes : 2 * modes] / math.sqrt(window)
    for s in range(2):
        residue_ref[s] = (jnp.sum(total_ref[s], axis=1) * scale).astype(BF16)


def residue_pass(doc_lengths, doc_streams, coef, grad_out, x_cols, arriving, window):
    tokens, chans = grad_out.shape
    modes = arriving.shape[1] // SEGS
    kinds = state_scratch(doc_lengths.shape[0], modes, tokens, chans)

    def kernel(*refs):
        residue_kernel(window, *refs)

    return call(
        kernel,
        [jax.ShapeDtypeStruct((2, modes, chans), BF16)],
        [kinds[k] for k in ("wide", "wide", "total", "order", "cuts")],
        "residue_pass",
        cost(4 * tokens * chans * modes, 4 * tokens * chans),
        [pltpu.SMEM] * 2 + [pltpu.VMEM] * 4,
        [pltpu.VMEM],
        (doc_lengths, doc_streams, coef, grad_out, x_cols, arriving),
    )[0]


def from_later(value, axis):
    count = lax.axis_size(axis)
    return [
        lax.ppermute(value, axis, [((i + k) % count, i) for i in range(count)])
        for k in range(1, count // 2 + 1)
    ]


def sum_over(value, axis):
    count = lax.axis_size(axis)
    half = count // 2
    parts = [value] + [
        lax.ppermute(value, axis, [(i, i // half * half + (i + k) % half) for i in range(count)])
        for k in range(1, half)
    ]
    parts = [part.astype(F32) for part in parts]
    while len(parts) > 1:
        middle = len(parts) // 2
        parts = [a + b for a, b in zip(parts[:middle], parts[middle:])]
    other = lax.ppermute(parts[0], axis, [(i, (i + half) % count) for i in range(count)])
    return parts[0] + other


def local(u_rows, gain, skip, residues, rates, grad_out, doc_lengths, doc_streams):
    ctx, groups = lax.axis_size("ctx"), lax.axis_size("ch")
    tokens, chans = grad_out.shape
    gain = gain[None, :]
    rates, residues = rates.T, residues.T
    x_send = norm_rows(u_rows, gain, groups)
    x_send, rates = lax.optimization_barrier((x_send, rates))
    x_cols = lax.all_to_all(x_send, "ch", split_axis=0, concat_axis=0, tiled=True)
    x_cols = x_cols.reshape(tokens, chans)
    seg_leaving, dev_leaving, coef = leave(
        doc_lengths, doc_streams, rates, residues, skip[None, :], grad_out
    )
    later = from_later(dev_leaving, "ctx")
    x_cols, *later = lax.optimization_barrier((x_cols, *later))
    normed_grad, arriving = back_pass(
        doc_lengths, doc_streams, rates, coef, grad_out, seg_leaving, later
    )
    grad_rows = lax.all_to_all(
        normed_grad.reshape(groups, tokens // groups, chans), "ch", split_axis=0, concat_axis=0, tiled=True
    )
    parts = residue_pass(doc_lengths, doc_streams, coef, grad_out, x_cols, arriving, tokens * ctx)
    residue_grad = sum_over(parts, "ctx").transpose(0, 2, 1)
    input_grad = final_rows(u_rows, gain, grad_rows)
    return (input_grad, residue_grad)


def solution(mesh):
    return jax.shard_map(
        local,
        mesh=mesh,
        in_specs=(
            P(("ctx", "ch"), None),
            P(),
            P("ch"),
            P("ch", None),
            P("ch", None),
            P("ctx", "ch"),
            P(),
            P(),
        ),
        out_specs=(P(("ctx", "ch"), None), P(None, "ch", None)),
        check_vma=False,
    )
```

```python
import math

import jax
import jax.numpy as jnp
from jax import lax
from jax.experimental import pallas as pl
from jax.experimental.pallas import tpu as pltpu
from jax.sharding import PartitionSpec as P

F32 = jnp.float32
BF16 = jnp.bfloat16
SEGS = 8
LANES = 128
UNROLL = 8
PIECES = 4
CHUNK = 256
ROW_BLOCK = 16


def cost(flops, size):
    return pl.CostEstimate(flops=flops, bytes_accessed=size, transcendentals=0)


def load(pairs, sems):
    copies = [pltpu.make_async_copy(a, b, sems.at[k]) for k, (a, b) in enumerate(pairs)]
    for copy in copies:
        copy.start()
    return copies


def call(kernel, outs, scratch, name, estimate, spaces, out_spaces, operands, limit=16):
    return pl.pallas_call(
        kernel,
        in_specs=[pl.BlockSpec(memory_space=space) for space in spaces],
        out_specs=[pl.BlockSpec(memory_space=space) for space in out_spaces],
        out_shape=outs,
        scratch_shapes=scratch,
        compiler_params=pltpu.CompilerParams(vmem_limit_bytes=limit * 1024 * 1024),
        cost_estimate=estimate,
        name=name,
    )(*operands)


def inverse_rms(u_ref, eps=1e-05):
    rows, width = u_ref.shape
    total = jnp.zeros((rows, LANES), F32)
    for c in range(width // LANES):
        part = u_ref[:, c * LANES : (c + 1) * LANES].astype(F32)
        total = total + part * part
    return lax.rsqrt(jnp.sum(total, axis=1, keepdims=True) / width + eps)


def norm_kernel(u_hbm, gain_hbm, out_hbm, u_ref, gain_ref, out_ref, sems):
    blocks, groups, rows, chans = out_ref.shape
    span = [pl.ds(b * rows, rows) for b in range(blocks)]
    gain_copy, *u_copies = load(
        [(gain_hbm, gain_ref)] + [(u_hbm.at[span[b]], u_ref.at[b]) for b in range(blocks)], sems
    )
    gain_copy.wait()
    out_copies = []
    for b in range(blocks):
        u_copies[b].wait()
        inv = inverse_rms(u_ref.at[b])
        for c in range(groups):
            cols = slice(c * chans, (c + 1) * chans)
            normal = u_ref[b, :, cols].astype(F32) * inv
            out_ref[b, c] = (normal * gain_ref[:, cols]).astype(BF16)
        copy = pltpu.make_async_copy(out_ref.at[b], out_hbm.at[:, span[b]], sems.at[1 + blocks + b])
        copy.start()
        out_copies.append(copy)
    for copy in out_copies:
        copy.wait()


def norm_rows(u_rows, gain, groups):
    rows, width = u_rows.shape
    chans, blocks = width // groups, rows // ROW_BLOCK
    return call(
        norm_kernel,
        [jax.ShapeDtypeStruct((groups, rows, chans), BF16)],
        [
            pltpu.VMEM((blocks, ROW_BLOCK, width), BF16),
            pltpu.VMEM((1, width), F32),
            pltpu.VMEM((blocks, groups, ROW_BLOCK, chans), BF16),
            pltpu.SemaphoreType.DMA((1 + 2 * blocks,)),
        ],
        "norm_rows",
        cost(8 * rows * width, 4 * rows * width),
        [pl.ANY] * 2,
        [pl.ANY],
        (u_rows, gain),
        60,
    )[0]


def final_kernel(u_ref, gain_ref, grad_ref, out_hbm, out_ref, sems):
    blocks, rows, _ = out_ref.shape
    groups, _, chans = grad_ref.shape
    width = groups * chans
    out_copies = []
    for b in range(blocks):
        span = pl.ds(b * rows, rows)
        inv = inverse_rms(u_ref.at[span])
        total = jnp.zeros((rows, chans), F32)
        for c in range(groups):
            cols = slice(c * chans, (c + 1) * chans)
            normal = u_ref[span, cols].astype(F32) * inv
            total = total + normal * (gain_ref[:, cols] * grad_ref[c, span, :].astype(F32))
        project = jnp.sum(total, axis=1, keepdims=True) / width
        for c in range(groups):
            cols = slice(c * chans, (c + 1) * chans)
            normal = u_ref[span, cols].astype(F32) * inv
            scaled = gain_ref[:, cols] * grad_ref[c, span, :].astype(F32)
            out_ref[b, :, cols] = (inv * (scaled - normal * project)).astype(BF16)
        copy = pltpu.make_async_copy(out_ref.at[b], out_hbm.at[span], sems.at[b])
        copy.start()
        out_copies.append(copy)
    for copy in out_copies:
        copy.wait()


def final_rows(u_rows, gain, grad_rows):
    rows, width = u_rows.shape
    blocks = rows // ROW_BLOCK
    return call(
        final_kernel,
        [jax.ShapeDtypeStruct((rows, width), BF16)],
        [
            pltpu.VMEM((blocks, ROW_BLOCK, width), BF16),
            pltpu.SemaphoreType.DMA((blocks,)),
        ],
        "final_rows",
        cost(16 * rows * width, 6 * rows * width),
        [pltpu.VMEM] * 3,
        [pl.ANY],
        (u_rows, gain, grad_rows),
    )[0]


def doc_starts(lens_ref):
    starts, at = [], jnp.int32(0)
    for k in range(lens_ref.shape[0] - 1):
        at = at + lens_ref[k]
        starts.append(at)
    return starts


def sort_down(codes):
    codes = list(codes)
    for end in range(len(codes) - 1, 0, -1):
        for k in range(end):
            high = jnp.maximum(codes[k], codes[k + 1])
            low = jnp.minimum(codes[k], codes[k + 1])
            codes[k], codes[k + 1] = high, low
    return codes


def cut_codes(starts, streams, base, seg_len):
    codes = []
    for start, stream in zip(starts, streams):
        place = start - base
        inside = (place >= 0) & (place < SEGS * seg_len)
        code = (place % seg_len) * 16 + place // seg_len
        codes.append(jnp.where(inside, code, 15) * 2 + stream)
    return sort_down(codes)


def any_start(starts, first, count):
    found = jnp.bool_(False)
    for start in starts:
        found = found | ((start >= first) & (start < first + count))
    return found


def time_loop(cuts_ref, seg_len, step, cut, carry):
    def piece(p, state):
        top, inner = state
        code = cuts_ref[p]
        low = code // 32
        count = top - low
        full = count // UNROLL

        def many(k, value):
            first = top - (k + 1) * UNROLL
            for j in range(UNROLL - 1, -1, -1):
                value = step(first + j, value)
            return value

        def one(k, value):
            return step(top - full * UNROLL - 1 - k, value)

        inner = lax.fori_loop(0, full, many, inner)
        inner = lax.fori_loop(0, count - full * UNROLL, one, inner)
        inner = cut((code // 2) % 16, code % 2, inner)
        return (low, inner)

    return lax.fori_loop(0, cuts_ref.shape[0], piece, (jnp.int32(seg_len), carry))[1]


def widen(source_ref, target_ref):
    halves, tokens, _ = target_ref.shape
    chunk = min(CHUNK, tokens)

    def body(j, _):
        rows = pl.ds(pl.multiple_of(j * chunk, chunk), chunk)
        for h in range(halves):
            target_ref[h, rows, :] = source_ref[rows, h * LANES : (h + 1) * LANES].astype(F32)
        return 0

    lax.fori_loop(0, tokens // chunk, body, 0)


def narrow_out(source_ref, target_ref, out_hbm, sems):
    halves, tokens, _ = source_ref.shape
    chunk = tokens // PIECES
    copies = []
    for k in range(PIECES):
        rows = pl.ds(k * chunk, chunk)
        for h in range(halves):
            target_ref[rows, h * LANES : (h + 1) * LANES] = source_ref[h, rows, :].astype(BF16)
        copies.append(pltpu.make_async_copy(target_ref.at[rows], out_hbm.at[rows], sems.at[k]))
        copies[-1].start()
    return copies


def step_rows(i, seg_len):
    return pl.ds(i, SEGS, stride=seg_len)


def spread(ref, r, cols):
    return jnp.broadcast_to(ref[r : r + 1, cols], (SEGS, LANES))


def segment(ref, s, modes):
    rows = slice(s * modes, (s + 1) * modes)
    return jnp.concatenate([ref[h, rows, :] for h in range(ref.shape[0])], axis=1)


def put_segment(ref, s, modes, value):
    for h in range(ref.shape[0]):
        ref[h, s * modes : (s + 1) * modes, :] = value[:, h * LANES : (h + 1) * LANES]


def store_cuts(cuts_ref, codes):
    for k, code in enumerate(codes):
        cuts_ref[k] = code
    cuts_ref[len(codes)] = jnp.int32(30)


def leave_kernel(
    lens_ref, streams_ref, rates_ref, residues_ref, skip_ref, grad_ref, seg_ref, dev_ref, coef_ref,
    wide_ref, cuts_ref,
):
    tokens, chans = grad_ref.shape
    modes = rates_ref.shape[0]
    seg_len = tokens // SEGS
    base = lax.axis_index("ctx") * tokens
    starts = doc_starts(lens_ref)
    streams = [streams_ref[k] for k in range(len(starts) + 1)]
    store_cuts(cuts_ref, cut_codes(starts, streams[1:], base, seg_len))
    widen(grad_ref, wide_ref)
    rates = rates_ref[...]
    decay_all = jnp.exp(-rates)
    mode_scale = jnp.sqrt(1.0 - decay_all * decay_all)
    coef_ref[:modes] = decay_all
    coef_ref[modes : 2 * modes] = mode_scale
    coef_ref[2 * modes : 3 * modes] = residues_ref[...] * mode_scale
    coef_ref[3 * modes :] = jnp.broadcast_to(skip_ref[...], (SEGS, chans))
    row = lax.broadcasted_iota(jnp.int32, (SEGS, LANES), 0)
    for h in range(chans // LANES):
        cols = slice(h * LANES, (h + 1) * LANES)
        decay = [spread(coef_ref, r, cols) for r in range(modes)]

        def step(i, state):
            grad = wide_ref[h, step_rows(i, seg_len), :]
            return tuple(grad + decay[r] * state[r] for r in range(modes))

        def cut(place, stream, state):
            hold = row != place
            return tuple(jnp.where(hold, part, 0.0) for part in state)

        zero = jnp.zeros((SEGS, LANES), F32)
        state = time_loop(cuts_ref, seg_len, step, cut, (zero,) * modes)
        for r in range(modes):
            seg_ref[h, pl.ds(r, SEGS, stride=modes), :] = decay[r] * state[r]
    through = jnp.exp(-rates * float(seg_len))
    leaving = segment(seg_ref, SEGS - 1, modes)
    for s in range(SEGS - 2, -1, -1):
        kept = jnp.where(any_start(starts, base + s * seg_len, seg_len), 0.0, 1.0)
        leaving = segment(seg_ref, s, modes) + (through * kept) * leaving
    dev_ref[...] = leaving


def state_scratch(docs, modes, tokens, chans):
    halves = chans // LANES
    return {
        "cuts": pltpu.SMEM((docs,), jnp.int32),
        "narrow": pltpu.VMEM((tokens, chans), BF16),
        "wide": pltpu.VMEM((halves, tokens, LANES), F32),
        "segs": pltpu.VMEM((halves, SEGS * modes, LANES), F32),
        "weights": pltpu.VMEM((modes, SEGS, LANES), F32),
        "total": pltpu.VMEM((2, modes, SEGS, chans), F32),
        "sems": pltpu.SemaphoreType.DMA((PIECES,)),
    }


def leave(doc_lengths, doc_streams, rates, residues, skip, grad_out):
    modes, chans = rates.shape
    tokens = grad_out.shape[0]
    kinds = state_scratch(doc_lengths.shape[0], modes, tokens, chans)
    return call(
        leave_kernel,
        [
            jax.ShapeDtypeStruct((chans // LANES, SEGS * modes, LANES), F32),
            jax.ShapeDtypeStruct((modes, chans), F32),
            jax.ShapeDtypeStruct((3 * modes + SEGS, chans), F32),
        ],
        [kinds[k] for k in ("wide", "cuts")],
        "leave",
        cost(2 * tokens * chans * modes, 2 * tokens * chans),
        [pltpu.SMEM] * 2 + [pltpu.VMEM] * 4,
        [pltpu.VMEM] * 3,
        (doc_lengths, doc_streams, rates, residues, skip, grad_out),
    )


def back_kernel(window, lens_ref, streams_ref, rates_ref, coef_ref, grad_ref, x_ref, seg_ref, *refs):
    later = refs[:-11]
    (out_hbm, residue_ref, out_ref, arrive_ref, wide_ref, x_wide_ref, conv_ref, weight_ref, total_ref,
     cuts_ref, sems) = refs[-11:]
    tokens, chans = grad_ref.shape
    modes = rates_ref.shape[0]
    seg_len = tokens // SEGS
    here, last = lax.axis_index("ctx"), lax.axis_size("ctx")
    base = here * tokens
    starts = doc_starts(lens_ref)
    streams = [streams_ref[k] for k in range(len(starts) + 1)]
    store_cuts(cuts_ref, cut_codes(starts, streams[1:], base, seg_len))
    rates = rates_ref[...]
    through = jnp.exp(-rates * float(tokens))
    arriving = jnp.zeros((modes, chans), F32)
    for k in range(len(later), 0, -1):
        kept = jnp.where(any_start(starts, (here + k) * tokens, tokens), 0.0, 1.0)
        arriving = later[k - 1][...] + (through * kept) * arriving
        arriving = jnp.where(here + k < last, arriving, 0.0)
    through = jnp.exp(-rates * float(seg_len))
    put_segment(arrive_ref, SEGS - 1, modes, arriving)
    for s in range(SEGS - 1, 0, -1):
        kept = jnp.where(any_start(starts, base + s * seg_len, seg_len), 0.0, 1.0)
        arriving = segment(seg_ref, s, modes) + (through * kept) * arriving
        put_segment(arrive_ref, s - 1, modes, arriving)
    widen(grad_ref, wide_ref)
    widen(x_ref, x_wide_ref)
    total_ref[...] = jnp.zeros_like(total_ref)
    row = lax.broadcasted_iota(jnp.int32, (SEGS, LANES), 0)
    first = base + row * seg_len
    stream_at = jnp.full((SEGS, LANES), streams[0], jnp.int32)
    for start, stream in zip(starts, streams[1:]):
        stream_at = jnp.where(first >= start, stream, stream_at)
    for h in range(chans // LANES):
        cols = slice(h * LANES, (h + 1) * LANES)
        decay = [spread(coef_ref, r, cols) for r in range(modes)]
        for r in range(modes):
            weight_ref[r] = spread(coef_ref, 2 * modes + r, cols)
        skip = coef_ref[3 * modes :, cols]

        def step(i, carry):
            state, total = carry
            rows = step_rows(i, seg_len)
            grad = wide_ref[h, rows, :]
            x = x_wide_ref[h, rows, :]
            sums = [skip * grad, None, None, None]
            new_state, new_total = [], []
            for r in range(modes):
                back = grad + state[r]
                term = weight_ref[r] * back
                sums[r % 4] = term if sums[r % 4] is None else sums[r % 4] + term
                new_total.append(total[r] + x * back)
                new_state.append(decay[r] * back)
            conv_ref[h, rows, :] = (sums[0] + sums[1]) + (sums[2] + sums[3])
            return (tuple(new_state), tuple(new_total))

        def cut(place, stream, carry):
            state, total = carry
            hold = row != place
            for r in range(modes):
                total_ref[stream, r, :, cols] += jnp.where(hold, 0.0, total[r])
            return (
                tuple(jnp.where(hold, part, 0.0) for part in state),
                tuple(jnp.where(hold, part, 0.0) for part in total),
            )

        zero = jnp.zeros((SEGS, LANES), F32)
        entry = tuple(arrive_ref[h, pl.ds(r, SEGS, stride=modes), :] for r in range(modes))
        _, total = time_loop(cuts_ref, seg_len, step, cut, (entry, (zero,) * modes))
        for s in range(2):
            for r in range(modes):
                total_ref[s, r, :, cols] += jnp.where(stream_at == s, total[r], 0.0)
    copies = narrow_out(conv_ref, out_ref, out_hbm, sems)
    scale = coef_ref[modes : 2 * modes] / math.sqrt(window)
    for s in range(2):
        residue_ref[s] = (jnp.sum(total_ref[s], axis=1) * scale).astype(BF16)
    for copy in copies:
        copy.wait()


def back_pass(doc_lengths, doc_streams, rates, coef, grad_out, x_cols, seg_leaving, later, window):
    modes, chans = rates.shape
    tokens = grad_out.shape[0]
    kinds = state_scratch(doc_lengths.shape[0], modes, tokens, chans)
    names = ("narrow", "segs", "wide", "wide", "wide", "weights", "total", "cuts", "sems")

    def kernel(*refs):
        back_kernel(window, *refs)

    return call(
        kernel,
        [
            jax.ShapeDtypeStruct((tokens, chans), BF16),
            jax.ShapeDtypeStruct((2, modes, chans), BF16),
        ],
        [kinds[k] for k in names],
        "back_pass",
        cost(6 * tokens * chans * modes, 6 * tokens * chans),
        [pltpu.SMEM] * 2 + [pltpu.VMEM] * (5 + len(later)),
        [pl.ANY, pltpu.VMEM],
        (doc_lengths, doc_streams, rates, coef, grad_out, x_cols, seg_leaving, *later),
        24,
    )


def from_later(value, axis):
    count = lax.axis_size(axis)
    return [
        lax.ppermute(value, axis, [((i + k) % count, i) for i in range(count)])
        for k in range(1, count // 2 + 1)
    ]


def sum_over(value, axis):
    count = lax.axis_size(axis)
    half = count // 2
    parts = [value] + [
        lax.ppermute(value, axis, [(i, i // half * half + (i + k) % half) for i in range(count)])
        for k in range(1, half)
    ]
    parts = [part.astype(F32) for part in parts]
    while len(parts) > 1:
        middle = len(parts) // 2
        parts = [a + b for a, b in zip(parts[:middle], parts[middle:])]
    other = lax.ppermute(parts[0], axis, [(i, (i + half) % count) for i in range(count)])
    return (parts[0], other)


def local(u_rows, gain, skip, residues, rates, grad_out, doc_lengths, doc_streams):
    ctx, groups = lax.axis_size("ctx"), lax.axis_size("ch")
    tokens, chans = grad_out.shape
    gain = gain[None, :]
    rates, residues = rates.T, residues.T
    x_send = norm_rows(u_rows, gain, groups)
    x_send, rates = lax.optimization_barrier((x_send, rates))
    x_cols = lax.all_to_all(x_send, "ch", split_axis=0, concat_axis=0, tiled=True)
    x_cols = x_cols.reshape(tokens, chans)
    seg_leaving, dev_leaving, coef = leave(
        doc_lengths, doc_streams, rates, residues, skip[None, :], grad_out
    )
    later = from_later(dev_leaving, "ctx")
    normed_grad, parts = back_pass(
        doc_lengths, doc_streams, rates, coef, grad_out, x_cols, seg_leaving, later, tokens * ctx
    )
    grad_rows = lax.all_to_all(
        normed_grad.reshape(groups, tokens // groups, chans), "ch", split_axis=0, concat_axis=0, tiled=True
    )
    mine, other = sum_over(parts, "ctx")
    input_grad = final_rows(u_rows, gain, grad_rows)
    other, input_grad = lax.optimization_barrier((other, input_grad))
    residue_grad = (mine + other).transpose(0, 2, 1)
    return (input_grad, residue_grad)


def solution(mesh):
    return jax.shard_map(
        local,
        mesh=mesh,
        in_specs=(
            P(("ctx", "ch"), None),
            P(),
            P("ch"),
            P("ch", None),
            P("ch", None),
            P("ctx", "ch"),
            P(),
            P(),
        ),
        out_specs=(P(("ctx", "ch"), None), P(None, "ch", None)),
        check_vma=False,
    )
```

```python
import math

import jax
import jax.numpy as jnp
from jax import lax
from jax.experimental import pallas as pl
from jax.experimental.pallas import tpu as pltpu
from jax.sharding import PartitionSpec as P

F32 = jnp.float32
BF16 = jnp.bfloat16
SEGS = 8
LANES = 128
UNROLL = 16
PIECES = 4
CHUNK = 256
ROW_BLOCK = 16


def cost(flops, size):
    return pl.CostEstimate(flops=flops, bytes_accessed=size, transcendentals=0)


def load(pairs, sems):
    copies = [pltpu.make_async_copy(a, b, sems.at[k]) for k, (a, b) in enumerate(pairs)]
    for copy in copies:
        copy.start()
    return copies


def call(kernel, outs, scratch, name, estimate, spaces, out_spaces, operands, limit=16):
    return pl.pallas_call(
        kernel,
        in_specs=[pl.BlockSpec(memory_space=space) for space in spaces],
        out_specs=[pl.BlockSpec(memory_space=space) for space in out_spaces],
        out_shape=outs,
        scratch_shapes=scratch,
        compiler_params=pltpu.CompilerParams(vmem_limit_bytes=limit * 1024 * 1024),
        cost_estimate=estimate,
        name=name,
    )(*operands)


def inverse_rms(u_ref, eps=1e-05):
    rows, width = u_ref.shape
    total = jnp.zeros((rows, LANES), F32)
    for c in range(width // LANES):
        part = u_ref[:, c * LANES : (c + 1) * LANES].astype(F32)
        total = total + part * part
    return lax.rsqrt(jnp.sum(total, axis=1, keepdims=True) / width + eps)


def norm_kernel(u_hbm, gain_hbm, out_hbm, u_ref, gain_ref, out_ref, sems):
    blocks, groups, rows, chans = out_ref.shape
    span = [pl.ds(b * rows, rows) for b in range(blocks)]
    gain_copy, *u_copies = load(
        [(gain_hbm, gain_ref)] + [(u_hbm.at[span[b]], u_ref.at[b]) for b in range(blocks)], sems
    )
    gain_copy.wait()
    out_copies = []
    for b in range(blocks):
        u_copies[b].wait()
        inv = inverse_rms(u_ref.at[b])
        for c in range(groups):
            cols = slice(c * chans, (c + 1) * chans)
            normal = u_ref[b, :, cols].astype(F32) * inv
            out_ref[b, c] = (normal * gain_ref[:, cols]).astype(BF16)
        copy = pltpu.make_async_copy(out_ref.at[b], out_hbm.at[:, span[b]], sems.at[1 + blocks + b])
        copy.start()
        out_copies.append(copy)
    for copy in out_copies:
        copy.wait()


def norm_rows(u_rows, gain, groups):
    rows, width = u_rows.shape
    chans, blocks = width // groups, rows // ROW_BLOCK
    return call(
        norm_kernel,
        [jax.ShapeDtypeStruct((groups, rows, chans), BF16)],
        [
            pltpu.VMEM((blocks, ROW_BLOCK, width), BF16),
            pltpu.VMEM((1, width), F32),
            pltpu.VMEM((blocks, groups, ROW_BLOCK, chans), BF16),
            pltpu.SemaphoreType.DMA((1 + 2 * blocks,)),
        ],
        "norm_rows",
        cost(8 * rows * width, 4 * rows * width),
        [pl.ANY] * 2,
        [pl.ANY],
        (u_rows, gain),
        60,
    )[0]


def final_kernel(u_ref, gain_ref, grad_ref, out_hbm, out_ref, sems):
    blocks, rows, _ = out_ref.shape
    groups, _, chans = grad_ref.shape
    width = groups * chans
    out_copies = []
    for b in range(blocks):
        span = pl.ds(b * rows, rows)
        inv = inverse_rms(u_ref.at[span])
        total = jnp.zeros((rows, chans), F32)
        for c in range(groups):
            cols = slice(c * chans, (c + 1) * chans)
            normal = u_ref[span, cols].astype(F32) * inv
            total = total + normal * (gain_ref[:, cols] * grad_ref[c, span, :].astype(F32))
        project = jnp.sum(total, axis=1, keepdims=True) / width
        for c in range(groups):
            cols = slice(c * chans, (c + 1) * chans)
            normal = u_ref[span, cols].astype(F32) * inv
            scaled = gain_ref[:, cols] * grad_ref[c, span, :].astype(F32)
            out_ref[b, :, cols] = (inv * (scaled - normal * project)).astype(BF16)
        copy = pltpu.make_async_copy(out_ref.at[b], out_hbm.at[span], sems.at[b])
        copy.start()
        out_copies.append(copy)
    for copy in out_copies:
        copy.wait()


def final_rows(u_rows, gain, grad_rows):
    rows, width = u_rows.shape
    blocks = rows // ROW_BLOCK
    return call(
        final_kernel,
        [jax.ShapeDtypeStruct((rows, width), BF16)],
        [
            pltpu.VMEM((blocks, ROW_BLOCK, width), BF16),
            pltpu.SemaphoreType.DMA((blocks,)),
        ],
        "final_rows",
        cost(16 * rows * width, 6 * rows * width),
        [pltpu.VMEM] * 3,
        [pl.ANY],
        (u_rows, gain, grad_rows),
    )[0]


def doc_starts(lens_ref):
    starts, at = [], jnp.int32(0)
    for k in range(lens_ref.shape[0] - 1):
        at = at + lens_ref[k]
        starts.append(at)
    return starts


def sort_down(codes):
    codes = list(codes)
    for end in range(len(codes) - 1, 0, -1):
        for k in range(end):
            high = jnp.maximum(codes[k], codes[k + 1])
            low = jnp.minimum(codes[k], codes[k + 1])
            codes[k], codes[k + 1] = high, low
    return codes


def cut_codes(starts, streams, base, seg_len):
    codes = []
    for start, stream in zip(starts, streams):
        place = start - base
        inside = (place >= 0) & (place < SEGS * seg_len)
        code = (place % seg_len) * 16 + place // seg_len
        codes.append(jnp.where(inside, code, 15) * 2 + stream)
    return sort_down(codes)


def any_start(starts, first, count):
    found = jnp.bool_(False)
    for start in starts:
        found = found | ((start >= first) & (start < first + count))
    return found


def time_loop(cuts_ref, seg_len, step, cut, carry):
    def piece(p, state):
        top, inner = state
        code = cuts_ref[p]
        low = code // 32
        count = top - low
        full = count // UNROLL

        def many(k, value):
            first = top - (k + 1) * UNROLL
            for j in range(UNROLL - 1, -1, -1):
                value = step(first + j, value)
            return value

        def one(k, value):
            return step(top - full * UNROLL - 1 - k, value)

        inner = lax.fori_loop(0, full, many, inner)
        inner = lax.fori_loop(0, count - full * UNROLL, one, inner)
        inner = cut((code // 2) % 16, code % 2, inner)
        return (low, inner)

    return lax.fori_loop(0, cuts_ref.shape[0], piece, (jnp.int32(seg_len), carry))[1]


def widen(source_ref, target_ref):
    halves, tokens, _ = target_ref.shape
    chunk = min(CHUNK, tokens)

    def body(j, _):
        rows = pl.ds(pl.multiple_of(j * chunk, chunk), chunk)
        for h in range(halves):
            target_ref[h, rows, :] = source_ref[rows, h * LANES : (h + 1) * LANES].astype(F32)
        return 0

    lax.fori_loop(0, tokens // chunk, body, 0)


def narrow_out(source_ref, target_ref, out_hbm, sems):
    halves, tokens, _ = source_ref.shape
    chunk = tokens // PIECES
    copies = []
    for k in range(PIECES):
        rows = pl.ds(k * chunk, chunk)
        for h in range(halves):
            target_ref[rows, h * LANES : (h + 1) * LANES] = source_ref[h, rows, :].astype(BF16)
        copies.append(pltpu.make_async_copy(target_ref.at[rows], out_hbm.at[rows], sems.at[k]))
        copies[-1].start()
    return copies


def step_rows(i, seg_len):
    return pl.ds(i, SEGS, stride=seg_len)


def spread(ref, r, cols):
    return jnp.broadcast_to(ref[r : r + 1, cols], (SEGS, LANES))


def segment(ref, s, modes):
    rows = slice(s * modes, (s + 1) * modes)
    return jnp.concatenate([ref[h, rows, :] for h in range(ref.shape[0])], axis=1)


def put_segment(ref, s, modes, value):
    for h in range(ref.shape[0]):
        ref[h, s * modes : (s + 1) * modes, :] = value[:, h * LANES : (h + 1) * LANES]


def store_cuts(cuts_ref, codes):
    for k, code in enumerate(codes):
        cuts_ref[k] = code
    cuts_ref[len(codes)] = jnp.int32(30)


def leave_kernel(
    lens_ref, streams_ref, rates_ref, residues_ref, skip_ref, grad_ref, seg_ref, dev_ref, coef_ref,
    wide_ref, cuts_ref,
):
    tokens, chans = grad_ref.shape
    modes = rates_ref.shape[0]
    seg_len = tokens // SEGS
    base = lax.axis_index("ctx") * tokens
    starts = doc_starts(lens_ref)
    streams = [streams_ref[k] for k in range(len(starts) + 1)]
    store_cuts(cuts_ref, cut_codes(starts, streams[1:], base, seg_len))
    widen(grad_ref, wide_ref)
    rates = rates_ref[...]
    decay_all = jnp.exp(-rates)
    mode_scale = jnp.sqrt(1.0 - decay_all * decay_all)
    coef_ref[:modes] = decay_all
    coef_ref[modes : 2 * modes] = mode_scale
    coef_ref[2 * modes : 3 * modes] = residues_ref[...] * mode_scale
    coef_ref[3 * modes :] = jnp.broadcast_to(skip_ref[...], (SEGS, chans))
    row = lax.broadcasted_iota(jnp.int32, (SEGS, LANES), 0)
    for h in range(chans // LANES):
        cols = slice(h * LANES, (h + 1) * LANES)
        decay = [spread(coef_ref, r, cols) for r in range(modes)]

        def step(i, state):
            grad = wide_ref[h, step_rows(i, seg_len), :]
            return tuple(grad + decay[r] * state[r] for r in range(modes))

        def cut(place, stream, state):
            hold = row != place
            return tuple(jnp.where(hold, part, 0.0) for part in state)

        zero = jnp.zeros((SEGS, LANES), F32)
        state = time_loop(cuts_ref, seg_len, step, cut, (zero,) * modes)
        for r in range(modes):
            seg_ref[h, pl.ds(r, SEGS, stride=modes), :] = decay[r] * state[r]
    through = jnp.exp(-rates * float(seg_len))
    leaving = segment(seg_ref, SEGS - 1, modes)
    for s in range(SEGS - 2, -1, -1):
        kept = jnp.where(any_start(starts, base + s * seg_len, seg_len), 0.0, 1.0)
        leaving = segment(seg_ref, s, modes) + (through * kept) * leaving
    dev_ref[...] = leaving


def state_scratch(docs, modes, tokens, chans):
    halves = chans // LANES
    return {
        "cuts": pltpu.SMEM((docs,), jnp.int32),
        "narrow": pltpu.VMEM((tokens, chans), BF16),
        "wide": pltpu.VMEM((halves, tokens, LANES), F32),
        "segs": pltpu.VMEM((halves, SEGS * modes, LANES), F32),
        "weights": pltpu.VMEM((modes, SEGS, LANES), F32),
        "total": pltpu.VMEM((2, modes, SEGS, chans), F32),
        "sems": pltpu.SemaphoreType.DMA((PIECES,)),
    }


def leave(doc_lengths, doc_streams, rates, residues, skip, grad_out):
    modes, chans = rates.shape
    tokens = grad_out.shape[0]
    kinds = state_scratch(doc_lengths.shape[0], modes, tokens, chans)
    return call(
        leave_kernel,
        [
            jax.ShapeDtypeStruct((chans // LANES, SEGS * modes, LANES), F32),
            jax.ShapeDtypeStruct((modes, chans), F32),
            jax.ShapeDtypeStruct((3 * modes + SEGS, chans), F32),
        ],
        [kinds[k] for k in ("wide", "cuts")],
        "leave",
        cost(2 * tokens * chans * modes, 2 * tokens * chans),
        [pltpu.SMEM] * 2 + [pltpu.VMEM] * 4,
        [pltpu.VMEM] * 3,
        (doc_lengths, doc_streams, rates, residues, skip, grad_out),
    )


def back_kernel(window, lens_ref, streams_ref, rates_ref, coef_ref, grad_ref, x_ref, seg_ref, *refs):
    later = refs[:-11]
    (out_hbm, residue_ref, out_ref, arrive_ref, wide_ref, x_wide_ref, conv_ref, weight_ref, total_ref,
     cuts_ref, sems) = refs[-11:]
    tokens, chans = grad_ref.shape
    modes = rates_ref.shape[0]
    seg_len = tokens // SEGS
    here, last = lax.axis_index("ctx"), lax.axis_size("ctx")
    base = here * tokens
    starts = doc_starts(lens_ref)
    streams = [streams_ref[k] for k in range(len(starts) + 1)]
    store_cuts(cuts_ref, cut_codes(starts, streams[1:], base, seg_len))
    rates = rates_ref[...]
    through = jnp.exp(-rates * float(tokens))
    arriving = jnp.zeros((modes, chans), F32)
    for k in range(len(later), 0, -1):
        kept = jnp.where(any_start(starts, (here + k) * tokens, tokens), 0.0, 1.0)
        arriving = later[k - 1][...] + (through * kept) * arriving
        arriving = jnp.where(here + k < last, arriving, 0.0)
    through = jnp.exp(-rates * float(seg_len))
    put_segment(arrive_ref, SEGS - 1, modes, arriving)
    for s in range(SEGS - 1, 0, -1):
        kept = jnp.where(any_start(starts, base + s * seg_len, seg_len), 0.0, 1.0)
        arriving = segment(seg_ref, s, modes) + (through * kept) * arriving
        put_segment(arrive_ref, s - 1, modes, arriving)
    widen(grad_ref, wide_ref)
    widen(x_ref, x_wide_ref)
    total_ref[...] = jnp.zeros_like(total_ref)
    row = lax.broadcasted_iota(jnp.int32, (SEGS, LANES), 0)
    first = base + row * seg_len
    stream_at = jnp.full((SEGS, LANES), streams[0], jnp.int32)
    for start, stream in zip(starts, streams[1:]):
        stream_at = jnp.where(first >= start, stream, stream_at)
    for h in range(chans // LANES):
        cols = slice(h * LANES, (h + 1) * LANES)
        decay = [spread(coef_ref, r, cols) for r in range(modes)]
        for r in range(modes):
            weight_ref[r] = spread(coef_ref, 2 * modes + r, cols)
        skip = coef_ref[3 * modes :, cols]

        def step(i, carry):
            state, total = carry
            rows = step_rows(i, seg_len)
            grad = wide_ref[h, rows, :]
            x = x_wide_ref[h, rows, :]
            sums = [skip * grad, None, None, None]
            new_state, new_total = [], []
            for r in range(modes):
                back = grad + state[r]
                term = weight_ref[r] * back
                sums[r % 4] = term if sums[r % 4] is None else sums[r % 4] + term
                new_total.append(total[r] + x * back)
                new_state.append(decay[r] * back)
            conv_ref[h, rows, :] = (sums[0] + sums[1]) + (sums[2] + sums[3])
            return (tuple(new_state), tuple(new_total))

        def cut(place, stream, carry):
            state, total = carry
            hold = row != place
            for r in range(modes):
                total_ref[stream, r, :, cols] += jnp.where(hold, 0.0, total[r])
            return (
                tuple(jnp.where(hold, part, 0.0) for part in state),
                tuple(jnp.where(hold, part, 0.0) for part in total),
            )

        zero = jnp.zeros((SEGS, LANES), F32)
        entry = tuple(arrive_ref[h, pl.ds(r, SEGS, stride=modes), :] for r in range(modes))
        _, total = time_loop(cuts_ref, seg_len, step, cut, (entry, (zero,) * modes))
        for s in range(2):
            for r in range(modes):
                total_ref[s, r, :, cols] += jnp.where(stream_at == s, total[r], 0.0)
    copies = narrow_out(conv_ref, out_ref, out_hbm, sems)
    scale = coef_ref[modes : 2 * modes] / math.sqrt(window)
    for s in range(2):
        residue_ref[s] = (jnp.sum(total_ref[s], axis=1) * scale).astype(BF16)
    for copy in copies:
        copy.wait()


def back_pass(doc_lengths, doc_streams, rates, coef, grad_out, x_cols, seg_leaving, later, window):
    modes, chans = rates.shape
    tokens = grad_out.shape[0]
    kinds = state_scratch(doc_lengths.shape[0], modes, tokens, chans)
    names = ("narrow", "segs", "wide", "wide", "wide", "weights", "total", "cuts", "sems")

    def kernel(*refs):
        back_kernel(window, *refs)

    return call(
        kernel,
        [
            jax.ShapeDtypeStruct((tokens, chans), BF16),
            jax.ShapeDtypeStruct((2, modes, chans), BF16),
        ],
        [kinds[k] for k in names],
        "back_pass",
        cost(6 * tokens * chans * modes, 6 * tokens * chans),
        [pltpu.SMEM] * 2 + [pltpu.VMEM] * (5 + len(later)),
        [pl.ANY, pltpu.VMEM],
        (doc_lengths, doc_streams, rates, coef, grad_out, x_cols, seg_leaving, *later),
        24,
    )


def from_later(value, axis):
    count = lax.axis_size(axis)
    return [
        lax.ppermute(value, axis, [((i + k) % count, i) for i in range(count)])
        for k in range(1, count // 2 + 1)
    ]


def sum_over(value, axis):
    count = lax.axis_size(axis)
    half = count // 2
    parts = [value] + [
        lax.ppermute(value, axis, [(i, i // half * half + (i + k) % half) for i in range(count)])
        for k in range(1, half)
    ]
    parts = [part.astype(F32) for part in parts]
    while len(parts) > 1:
        middle = len(parts) // 2
        parts = [a + b for a, b in zip(parts[:middle], parts[middle:])]
    other = lax.ppermute(parts[0], axis, [(i, (i + half) % count) for i in range(count)])
    return (parts[0], other)


def local(u_rows, gain, skip, residues, rates, grad_out, doc_lengths, doc_streams):
    ctx, groups = lax.axis_size("ctx"), lax.axis_size("ch")
    tokens, chans = grad_out.shape
    gain = gain[None, :]
    rates, residues = rates.T, residues.T
    x_send = norm_rows(u_rows, gain, groups)
    x_send, rates = lax.optimization_barrier((x_send, rates))
    x_cols = lax.all_to_all(x_send, "ch", split_axis=0, concat_axis=0, tiled=True)
    x_cols = x_cols.reshape(tokens, chans)
    seg_leaving, dev_leaving, coef = leave(
        doc_lengths, doc_streams, rates, residues, skip[None, :], grad_out
    )
    later = from_later(dev_leaving, "ctx")
    normed_grad, parts = back_pass(
        doc_lengths, doc_streams, rates, coef, grad_out, x_cols, seg_leaving, later, tokens * ctx
    )
    grad_rows = lax.all_to_all(
        normed_grad.reshape(groups, tokens // groups, chans), "ch", split_axis=0, concat_axis=0, tiled=True
    )
    mine, other = sum_over(parts, "ctx")
    input_grad = final_rows(u_rows, gain, grad_rows)
    other, input_grad = lax.optimization_barrier((other, input_grad))
    residue_grad = (mine + other).transpose(0, 2, 1)
    return (input_grad, residue_grad)


def solution(mesh):
    return jax.shard_map(
        local,
        mesh=mesh,
        in_specs=(
            P(("ctx", "ch"), None),
            P(),
            P("ch"),
            P("ch", None),
            P("ch", None),
            P("ctx", "ch"),
            P(),
            P(),
        ),
        out_specs=(P(("ctx", "ch"), None), P(None, "ch", None)),
        check_vma=False,
    )
```
